32 devices in a mesh: rx: 8 (over z, x), ry: 4 (over y, core).
Axes of the slice: x: 2, y: 2, z: 4, core: 2. Of those that a mesh axis runs over, the one named last changes fastest.
Arguments:
- cell_input: bfloat16 [32, 16, 64, 128], P('rx', 'ry'), may hold values from -6 to 6
- w_filter: bfloat16 [2, 32, 32], replicated, may hold values from -0.75 to 0.75
- w_gate: bfloat16 [2, 32, 32], replicated, may hold values from -0.75 to 0.75
- bias_filter: float32 [32], replicated, may hold values from -3 to 3
- bias_gate: float32 [32], replicated, may hold values from -3 to 3
- adjacency: bfloat16 [32, 16, 5, 4096], P('rx', 'ry'), may hold values from -0.3125 to 0.3125
- out_block: int32 [8, 4, 12], P('rx', 'ry'), may hold values from 0 to 15
- out_dev: int32 [8, 4, 12, 1], P('rx', 'ry'), may hold values from 0 to 7; in each aligned block of 12 rows (0 to 11, 12 to 23, ..., all dimensions but the last counted through in order) at most 2 rows name the same one
- out_target: int32 [8, 4, 12], P('rx', 'ry'), may hold values from 0 to 15
- out_tiles: bfloat16 [8, 4, 12, 4096], P('rx', 'ry'), may hold values from -0.75 to 0.75
- w_mix: bfloat16 [3, 32, 32], replicated, may hold values from -0.625 to 0.625
- bias_mix: float32 [32], replicated, may hold values from -3 to 3
Outputs:
- layer_output: bfloat16 [32, 16, 64, 128], P('rx', 'ry')
The draws below stay inside these ranges and needn't reach their ends.
Inputs may be any that keep to these rules, and one draw needn't show every extreme that they name: `out_dev`: among the 12 edges of one region no destination region row appears more than 2 times, and in some regions one appears exactly 2 times.
All inputs are finite; a program needn't handle non-finite values.
Results may differ from the reference program's by a relative error of at most 0.0045.
Values may be sent and summed in bfloat16 or wider, within the bound.
A program may use at most 64 MiB of HBM per device.

```python
import math
import jax
import jax.numpy as jnp
import numpy as np
from jax import lax

C = 32
BSZ = 64
DILATION_STEP = 2
BR = 4
BC = 4
CAP = 2
E_DEV = 12
GR = 32
GC = 16
F = 128
TILE = 4096
N_RX = 8
N_RY = 4


def with_ends(array, own_key, low, high):
    dims = array.shape
    spot = [jax.random.randint(jax.random.fold_in(own_key, axis), (), 0, dims[axis]) for axis in range(len(dims))]
    array = array.at[tuple(spot)].set(low)
    longest = dims.index(max(dims))
    spot[longest] = (spot[longest] + 1) % dims[longest]
    return array.at[tuple(spot)].set(high)


def shard_levels(rng, dims, cuts, smallest, high):
    level = 1.0
    for dim, blocks in cuts:
        heights = jax.random.uniform(jax.random.fold_in(jax.random.fold_in(rng, 6), dim), (blocks,), jnp.float32, smallest / len(cuts), high / len(cuts))
        level = level * jnp.repeat(jnp.exp(heights), dims[dim] // blocks).reshape((-1,) + (1,) * (len(dims) - 1 - dim))
    return level


def routed_block(key, own, number, rows, amount, top, bound, skew):
    ranking = jax.random.permutation(key, amount)
    heavy_load, ordinary = portions_of(amount, rows * top, bound, skew, True), portions_of(amount, rows * top, bound, skew, False)
    places = jnp.arange(amount)

    def named(tallies, turn):
        used = int((tallies > 0).sum())
        fixed = max(1, used // 4)
        shifted = fixed + (places - fixed + turn * (used - fixed)) % max(1, amount - fixed)
        return jnp.zeros((amount,), jnp.int32).at[ranking[jnp.where(places < fixed, places, shifted)]].set(jnp.asarray(tallies, jnp.int32))

    tallies = jnp.where(number % 4 == 0, named(heavy_load, number // 4), named(ordinary, number - number // 4 - 1))
    mixed = jax.random.permutation(jax.random.fold_in(own, 3), amount)
    donor, receiver = mixed[0:amount // 2 * 2:2], mixed[1:amount // 2 * 2:2]
    margin = jnp.minimum(tallies[donor] - 1, bound - tallies[receiver]) // 2
    margin = jnp.where((donor == ranking[0]) | (receiver == ranking[0]) | (tallies[receiver] == 0), 0, jnp.maximum(margin, 0))
    shifted = jax.random.randint(jax.random.fold_in(own, 4), (amount // 2,), 0, 1 << 20) % (margin + 1)
    tallies = tallies.at[donor].add(-shifted).at[receiver].add(shifted)
    items = jnp.searchsorted(jnp.cumsum(tallies), jnp.arange(rows * top), side="right").astype(jnp.int32)
    table = items.reshape(top, rows).T
    table = table[jax.random.permutation(jax.random.fold_in(own, 1), rows)]
    turn = jax.random.randint(jax.random.fold_in(own, 2), (rows, 1), 0, top)
    return jnp.take_along_axis(table, (jnp.arange(top)[None, :] + turn) % top, axis=1)


def portions_of(count, total, limit, lean, full):
    weights = [(1 << 20) // math.isqrt(rank ** lean) + 1 for rank in range(1, count + 1)]
    largest = limit if full else min(limit, max(-(-total // count), total * weights[0] // sum(weights)))
    least = 1 if total - largest >= count - 1 else 0
    holding, rest = [largest] + [least] * (count - 1), total - largest - least * (count - 1)
    while rest > 0:
        free = [i for i in range(1, count) if holding[i] < largest] or [i for i in range(1, count) if holding[i] < limit]
        mass, budget = sum([weights[i] for i in free]), rest
        for i in free:
            more = min(limit - holding[i], max(1, budget * weights[i] // mass), rest)
            holding[i] = holding[i] + more
            rest = rest - more
    return np.array(holding)


def scatter_about(key, extent, deviation, limit, pieces=(), kind=jnp.bfloat16):
    entries = jax.random.normal(key, extent, jnp.float32) * deviation
    if len(pieces) > 0:
        entries = shard_levels(key, extent, pieces, -0.22, 0.18) * entries
    return jnp.clip(entries, min=-limit, max=limit).astype(kind)


def setup_inputs(seed: int = 0) -> dict:
    seeds = jax.random.split(jax.random.key(seed), 13)
    cell_input = scatter_about(seeds[0], (GR, GC, BSZ, F), 1.0, 6.0, ((0, 8), (1, 4)))
    w_filter = scatter_about(seeds[1], (2, C, C), (2 * C) ** -0.5, 0.75)
    w_gate = scatter_about(seeds[2], (2, C, C), (2 * C) ** -0.5, 0.75)
    bias_filter = scatter_about(seeds[3], (C,), 0.5, 3.0, (), jnp.float32)
    bias_gate = scatter_about(seeds[4], (C,), 0.5, 3.0, (), jnp.float32)
    adjacency = scatter_about(seeds[5], (GR, GC, 5, TILE), (5 * BSZ) ** -0.5, 0.3125, ((0, 8), (1, 4)))
    out_block = with_ends(jax.random.randint(seeds[6], (N_RX, N_RY, E_DEV), 0, BR * BC), jax.random.fold_in(seeds[6], 1), 0, (BR * BC) - 1).astype(jnp.int32)
    out_dev_keys = jax.random.split(jax.random.fold_in(seeds[7], 1), N_RX * N_RY * E_DEV // E_DEV)
    out_dev_turns = jax.random.permutation(jax.random.fold_in(seeds[7], 3), N_RX * N_RY * E_DEV // E_DEV)
    out_dev = jax.vmap(lambda own, number: routed_block(jax.random.fold_in(seeds[7], 2), own, number, E_DEV, N_RX, 1, CAP, 2))(out_dev_keys, out_dev_turns).reshape((N_RX, N_RY, E_DEV, 1))
    out_target = with_ends(jax.random.randint(seeds[8], (N_RX, N_RY, E_DEV), 0, BR * BC), jax.random.fold_in(seeds[8], 1), 0, (BR * BC) - 1).astype(jnp.int32)
    out_tiles = scatter_about(seeds[9], (N_RX, N_RY, E_DEV, TILE), BSZ ** -0.5, 0.75, ((0, 8), (1, 4)))
    w_mix = scatter_about(seeds[10], (3, C, C), (3 * C) ** -0.5, 0.625)
    bias_mix = scatter_about(seeds[11], (C,), 0.5, 3.0, (), jnp.float32)
    return {"cell_input": cell_input, "w_filter": w_filter, "w_gate": w_gate, "bias_filter": bias_filter, "bias_gate": bias_gate, "adjacency": adjacency, "out_block": out_block, "out_dev": out_dev, "out_target": out_target, "out_tiles": out_tiles, "w_mix": w_mix, "bias_mix": bias_mix}


def temporal_units(cell_row, w_filter, w_gate, bias_filter, bias_gate):
    channels = w_filter.shape[1]
    current_step = cell_row.astype(jnp.float32).reshape(cell_row.shape[0], cell_row.shape[1], -1, channels)
    earlier_step = jnp.concatenate([jnp.zeros_like(current_step[:, :, :DILATION_STEP]), current_step[:, :, :-DILATION_STEP]], axis=2)
    filter_taps = w_filter.astype(jnp.float32)
    gate_taps = w_gate.astype(jnp.float32)
    pre_filter = jnp.einsum("nbtc,cd->nbtd", current_step, filter_taps[1]) + jnp.einsum("nbtc,cd->nbtd", earlier_step, filter_taps[0]) + bias_filter
    pre_gate = jnp.einsum("nbtc,cd->nbtd", current_step, gate_taps[1]) + jnp.einsum("nbtc,cd->nbtd", earlier_step, gate_taps[0]) + bias_gate
    gated = jnp.tanh(pre_filter) * jax.nn.sigmoid(pre_gate)
    return gated.astype(jnp.bfloat16).reshape(cell_row.shape)


def far_term(signal, out_block, out_dev, out_target, out_tiles):
    far_sum = jnp.zeros(signal.shape, jnp.float32)

    def add_sender(far_sum, sender):
        strip_rows = lax.dynamic_slice_in_dim(signal, sender * BR, BR, 0)
        blocks = strip_rows.reshape(BR, N_RY, BC, BSZ, F).transpose(1, 0, 2, 3, 4).reshape(N_RY, BR * BC, BSZ, F)
        chosen = out_block[sender]
        source_feats = jax.vmap(lambda region, picks: region[picks])(blocks, chosen)
        edge_tiles = out_tiles[sender].astype(jnp.float32).reshape(N_RY, E_DEV, BSZ, BSZ)
        products = jnp.einsum("qeab,qebf->qeaf", edge_tiles, source_feats.astype(jnp.float32))
        targets = out_target[sender]
        dest_rows = out_dev[sender, :, :, 0] * BR + targets // BC
        dest_cols = jnp.arange(N_RY, dtype=jnp.int32)[:, None] * BC + targets % BC
        far_sum = far_sum.at[dest_rows, dest_cols].add(products)
        return far_sum, None

    far_sum, unused = lax.scan(add_sender, far_sum, jnp.arange(N_RX, dtype=jnp.int32))
    return far_sum


def stencil_row(block_row, padded, adjacency, far_sum):
    neighbours = (padded[block_row + 1, 1:-1], padded[block_row, 1:-1], padded[block_row + 2, 1:-1],
                  padded[block_row + 1, :-2], padded[block_row + 1, 2:])
    adj_row = adjacency[block_row].astype(jnp.float32).reshape(GC, 5, BSZ, BSZ)
    row_sum = far_sum[block_row]
    for offset in range(5):
        row_sum = row_sum + jnp.einsum("jab,jbf->jaf", adj_row[:, offset], neighbours[offset].astype(jnp.float32))
    return row_sum


def mix_row(gated_row, first_row, second_row, w_mix, bias_mix):
    shape_four = (gated_row.shape[0], gated_row.shape[1], -1, w_mix.shape[1])
    weights = w_mix.astype(jnp.float32)
    mixture = jnp.einsum("jatc,cd->jatd", gated_row.astype(jnp.float32).reshape(shape_four), weights[0])
    mixture = mixture + jnp.einsum("jatc,cd->jatd", first_row.astype(jnp.float32).reshape(shape_four), weights[1])
    mixture = mixture + jnp.einsum("jatc,cd->jatd", second_row.reshape(shape_four), weights[2], precision=lax.Precision.HIGHEST)
    mixture = mixture + bias_mix
    return mixture.reshape(gated_row.shape)


def reference(cell_input, w_filter, w_gate, bias_filter, bias_gate, adjacency, out_block, out_dev, out_target, out_tiles, w_mix, bias_mix):
    gated = lax.map(lambda cell_row: temporal_units(cell_row, w_filter, w_gate, bias_filter, bias_gate), cell_input)
    padding = ((1, 1), (1, 1), (0, 0), (0, 0))
    row_ids = jnp.arange(GR, dtype=jnp.int32)
    far_one = far_term(gated, out_block, out_dev, out_target, out_tiles)
    padded_one = jnp.pad(gated, padding)
    first_hop = lax.map(lambda block_row: stencil_row(block_row, padded_one, adjacency, far_one).astype(jnp.bfloat16), row_ids)
    far_two = far_term(first_hop, out_block, out_dev, out_target, out_tiles)
    padded_two = jnp.pad(first_hop, padding)

    def finish(block_row):
        second_row = stencil_row(block_row, padded_two, adjacency, far_two)
        mixture = mix_row(gated[block_row], first_hop[block_row], second_row, w_mix, bias_mix)
        return (cell_input[block_row].astype(jnp.float32) + mixture).astype(jnp.bfloat16)

    return lax.map(finish, row_ids)
```

```python
import functools

import jax
import jax.numpy as jnp
from jax import lax
from jax.experimental import pallas as pl
from jax.experimental.pallas import tpu as pltpu
from jax.sharding import PartitionSpec as P

DILATION_STEP = 2
CAP = 2
MESH = pl.DeviceIdType.MESH
F32 = jnp.float32
BF16 = jnp.bfloat16


def dot(a, b):
    return jnp.dot(a, b, preferred_element_type=F32)


def each(count, body, limit=8):
    if count <= limit:
        for k in range(count):
            body(k)
    else:

        def step(k, carry):
            body(k)
            return carry

        lax.fori_loop(0, count, step, 0)


def blocks_loop(count, body, unroll):
    def step(k, carry):
        body(k)
        return carry

    lax.fori_loop(0, count, step, 0, unroll=unroll)


def kernel(
    n,
    ny,
    cell,
    w_filter,
    w_gate,
    bias_filter,
    bias_gate,
    adjacency,
    out_block,
    out_dev,
    out_target,
    out_tiles,
    w_mix,
    bias_mix,
    out,
    gated,
    first,
    halo_rows,
    halo_cols,
    send_buf,
    recv_buf,
    target_send,
    target_recv,
    select,
    tiles,
    edge_tiles,
    spread,
    edge_spread,
    table,
    bias_table,
    acc,
    base,
    send_sem,
    recv_sem,
    target_send_sem,
    target_recv_sem,
    halo_send_sem,
    halo_recv_sem,
):
    br, bc, size, feats = cell.shape
    blocks = br * bc
    rows = blocks * size
    half = size // 2
    edges = out_tiles.shape[2]
    channels = w_filter.shape[1]
    steps = feats // channels
    stride = edge_spread.shape[0] // half
    rx = lax.axis_index("rx")
    ry = lax.axis_index("ry")

    barrier = pltpu.get_barrier_semaphore()

    def greet(k):
        pl.semaphore_signal(
            barrier, inc=1, device_id={"rx": lax.rem(rx + k + 1, n)}, device_id_type=MESH
        )

    each(n - 1, greet)

    @pl.when(ry > 0)
    def _():
        pl.semaphore_signal(barrier, inc=1, device_id={"ry": ry - 1}, device_id_type=MESH)

    @pl.when(ry < ny - 1)
    def _():
        pl.semaphore_signal(barrier, inc=1, device_id={"ry": ry + 1}, device_id_type=MESH)

    zero_side = jnp.zeros((2,) + halo_rows.shape[2:], BF16)

    @pl.when(rx == 0)
    def _():
        halo_rows[:, 0] = zero_side

    @pl.when(rx == n - 1)
    def _():
        halo_rows[:, 1] = zero_side

    @pl.when(ry == 0)
    def _():
        halo_cols[:, 0] = zero_side

    @pl.when(ry == ny - 1)
    def _():
        halo_cols[:, 1] = zero_side

    table[...] = jnp.zeros_like(table)
    for t in range(steps):
        span = slice(t * channels, (t + 1) * channels)
        for which, weights in enumerate((w_filter, w_gate)):
            for tap, to in ((1, t), (0, t + DILATION_STEP)):
                if to < steps:
                    at = which * feats + to * channels
                    table[span, at : at + channels] = weights[tap].astype(F32)
        for hop in range(3):
            at = (2 + hop) * feats + t * channels
            table[span, at : at + channels] = w_mix[hop].astype(F32)
        bias_table[0:1, span] = bias_filter[...]
        bias_table[1:2, span] = bias_gate[...]
        bias_table[2:3, span] = bias_mix[...]
    taps = table[:, : 2 * feats].astype(BF16)
    mixes = [table[:, (2 + h) * feats : (3 + h) * feats].astype(BF16) for h in range(3)]

    for i in range(br):
        pre = dot(cell[i].reshape(bc * size, feats), taps)
        pre_f = pre[:, :feats] + bias_table[0:1]
        pre_g = pre[:, feats:] + bias_table[1:2]
        value = jnp.tanh(pre_f) * (0.5 * jnp.tanh(0.5 * pre_g) + 0.5)
        gated[i] = value.astype(BF16).reshape(bc, size, feats)

    for r in range(half):
        piece = out_tiles[0, 0, :, r * 2 * size : (r + 1) * 2 * size]
        edge_spread[r * stride : r * stride + edges] = piece.astype(F32)
    for e in range(edges):
        pairs = edge_spread[pl.ds(e, half, stride=stride), :]
        edge_tiles[e, :half] = pairs.astype(BF16)
        edge_tiles[e, half:] = pltpu.roll(pairs, size, 1).astype(BF16)

    def slots(d):
        head, tail = jnp.int32(-1), jnp.int32(-1)
        for e in range(edges):
            hit = out_dev[0, 0, e, 0] == d
            head = jnp.where(hit & (head < 0), e, head)
            tail = jnp.where(hit, e, tail)
        return ((jnp.maximum(head, 0), head >= 0), (jnp.maximum(tail, 0), tail != head))

    lane = lax.broadcasted_iota(jnp.int32, (8, CAP * size), 1)

    def halo_copies(signal, hop):
        sides = []
        for which, (axis, here, count, halo) in enumerate(
            (("rx", rx, n, halo_rows), ("ry", ry, ny, halo_cols))
        ):
            last = (br if which == 0 else bc) - 1
            for side, (edge, step) in enumerate(((last, 1), (0, -1))):
                src = signal.at[edge] if which == 0 else signal.at[:, edge]
                copy = pltpu.make_async_remote_copy(
                    src_ref=src,
                    dst_ref=halo.at[hop, side],
                    send_sem=halo_send_sem.at[hop, which, side],
                    recv_sem=halo_recv_sem.at[hop, which, side],
                    device_id={axis: jnp.clip(here + step, 0, count - 1)},
                    device_id_type=MESH,
                )
                sends = (here < count - 1) if step == 1 else (here > 0)
                gets = (here > 0) if step == 1 else (here < count - 1)
                sides.append((sends, gets, copy))
        return sides

    def far_copy(hop, d, source):
        return pltpu.make_async_remote_copy(
            src_ref=send_buf.at[hop, d],
            dst_ref=recv_buf.at[hop, source],
            send_sem=send_sem.at[hop, d],
            recv_sem=recv_sem.at[hop, source],
            device_id={"rx": d},
            device_id_type=MESH,
        )

    def target_copy(d, source):
        return pltpu.make_async_remote_copy(
            src_ref=target_send.at[d],
            dst_ref=target_recv.at[source],
            send_sem=target_send_sem.at[d],
            recv_sem=target_recv_sem.at[source],
            device_id={"rx": d},
            device_id_type=MESH,
        )

    def send_far(signal, hop):
        def one(k):
            d = lax.rem(rx + k + 1, n)
            products, targets = [], []
            for index, valid in slots(d):
                b = out_block[0, 0, index]
                block = signal[lax.div(b, bc), lax.rem(b, bc)]
                product = dot(edge_tiles[index][:, :size], block)
                products.append((product * jnp.where(valid, 1.0, 0.0)).astype(BF16))
                targets.append(jnp.where(valid, out_target[0, 0, index], -1))
            both = jnp.concatenate(products, axis=0)
            named = jnp.where(lane < size, targets[0], targets[1]).astype(F32)
            own = k == n - 1

            def keep():
                recv_buf[hop, rx] = both
                if hop == 0:
                    target_recv[rx] = named

            def send():
                send_buf[hop, d] = both
                far_copy(hop, d, rx).start()
                if hop == 0:
                    target_send[d] = named
                    target_copy(d, rx).start()

            if isinstance(own, bool):
                keep() if own else send()
            else:
                pl.when(own)(keep)
                pl.when(jnp.logical_not(own))(send)

        each(n, one)

    def wait_far(hop):
        def one(k):
            source = lax.rem(rx + n - k - 1, n)
            far_copy(hop, source, source).wait_recv()

        each(n - 1, one)

    def near(signal, hop):
        for i in range(br):
            for j in range(bc):
                up = signal[i - 1, j] if i > 0 else halo_rows[hop, 0, j]
                down = signal[i + 1, j] if i < br - 1 else halo_rows[hop, 1, j]
                left = signal[i, j - 1] if j > 0 else halo_cols[hop, 0, i]
                right = signal[i, j + 1] if j < bc - 1 else halo_cols[hop, 1, i]
                column = jnp.concatenate([signal[i, j], up, down, left, right], axis=0)
                total = dot(tiles[i * bc + j][:, : 5 * size], column)
                at = (i * bc + j) * size
                acc[pl.ds(at, half, stride=2), :] = total[:half]
                acc[pl.ds(at + 1, half, stride=2), :] = total[half:]

    pl.semaphore_wait(
        barrier,
        n - 1 + jnp.where(ry > 0, 1, 0) + jnp.where(ry < ny - 1, 1, 0),
    )

    def start_hop(signal, hop):
        for sends, gets, copy in halo_copies(signal, hop):
            pl.when(sends)(copy.start)
        send_far(signal, hop)

    def wait_halo(signal, hop):
        for sends, gets, copy in halo_copies(signal, hop):
            pl.when(gets)(copy.wait_recv)

    start_hop(gated, 0)

    low = lax.broadcasted_iota(jnp.int32, (half, 2 * size), 1) < size

    def arrange(ij):
        slot = lax.rem(ij, spread.shape[0])
        i, j = lax.div(ij, bc), lax.rem(ij, bc)
        for r in range(half):
            piece = adjacency[i, j, :, r * 2 * size : (r + 1) * 2 * size]
            spread[slot, r * 8 : r * 8 + 5] = piece.astype(F32)
        pairs = [spread[slot, pl.ds(k, half, stride=8), :] for k in range(5)]
        turned = [pltpu.roll(pair, size, 1) for pair in pairs]
        zero = jnp.zeros_like(pairs[0])
        pairs.append(zero)
        turned.append(zero)
        for k in range(0, 6, 2):
            span = slice(k * size, (k + 2) * size)
            tiles[ij, :half, span] = jnp.where(low, pairs[k], turned[k + 1]).astype(BF16)
            tiles[ij, half:, span] = jnp.where(low, turned[k], pairs[k + 1]).astype(BF16)

    blocks_loop(blocks, arrange, 4)

    wait_halo(gated, 0)
    near(gated, 0)

    def wait_target(k):
        source = lax.rem(rx + n - k - 1, n)
        target_copy(source, source).wait_recv()

    each(n - 1, wait_target)
    spot = lax.broadcasted_iota(jnp.int32, (size, CAP * size), 1) % size
    row = lax.broadcasted_iota(jnp.int32, (size, CAP * size), 0)
    unit = jnp.where(row == 2 * (spot % half) + spot // half, 1.0, 0.0).astype(BF16)
    for source in range(n):
        named = target_recv[source, 0:1]
        span = slice(source * CAP * size, (source + 1) * CAP * size)
        for block in range(blocks):
            hit = jnp.where(named == float(block), 1.0, 0.0).astype(BF16)
            select[block * size : (block + 1) * size, span] = unit * hit

    wait_far(0)
    landed = recv_buf[0].reshape(n * CAP * size, feats)
    strip = bc * size
    for i in range(br):
        total = acc[i * strip : (i + 1) * strip] + dot(select[i * strip : (i + 1) * strip], landed)
        first[i] = total.astype(BF16).reshape(bc, size, feats)

    start_hop(first, 1)

    for i in range(br):
        own = dot(gated[i].reshape(strip, feats), mixes[0])
        own = own + dot(first[i].reshape(strip, feats), mixes[1]) + bias_table[2:3]
        base[i * strip : (i + 1) * strip] = own + cell[i].reshape(strip, feats).astype(F32)
    wait_halo(first, 1)
    near(first, 1)

    wait_far(1)
    landed = recv_buf[1].reshape(n * CAP * size, feats)
    for i in range(br):
        span = slice(i * strip, (i + 1) * strip)
        second = acc[span] + dot(select[span], landed)
        upper = second.astype(BF16)
        lower = (second - upper.astype(F32)).astype(BF16)
        total = base[span] + (dot(upper, mixes[2]) + dot(lower, mixes[2]))
        out[i] = total.astype(BF16).reshape(bc, size, feats)

    for hop, signal in enumerate((gated, first)):
        for sends, gets, copy in halo_copies(signal, hop):
            pl.when(sends)(copy.wait_send)

        def sent(k):
            d = lax.rem(rx + k + 1, n)
            far_copy(hop, d, rx).wait_send()
            if hop == 0:
                target_copy(d, rx).wait_send()

        each(n - 1, sent)


def local(
    n,
    ny,
    cell_input,
    w_filter,
    w_gate,
    bias_filter,
    bias_gate,
    adjacency,
    out_block,
    out_dev,
    out_target,
    out_tiles,
    w_mix,
    bias_mix,
):
    br, bc, size, feats = cell_input.shape
    blocks = br * bc
    rows = blocks * size
    edges = out_tiles.shape[2]
    channels = w_filter.shape[1]
    half = size // 2
    stride = -(-edges // 8) * 8
    assert feats == 128 and size == 64 and br == bc
    vmem = pl.BlockSpec(memory_space=pltpu.VMEM)
    smem = pl.BlockSpec(memory_space=pltpu.SMEM)
    dma = pltpu.SemaphoreType.DMA
    scratch = [
        pltpu.VMEM((br, bc, size, feats), BF16),
        pltpu.VMEM((br, bc, size, feats), BF16),
        pltpu.VMEM((2, 2, bc, size, feats), BF16),
        pltpu.VMEM((2, 2, br, size, feats), BF16),
        pltpu.VMEM((2, n, CAP * size, feats), BF16),
        pltpu.VMEM((2, n, CAP * size, feats), BF16),
        pltpu.VMEM((n, 8, CAP * size), F32),
        pltpu.VMEM((n, 8, CAP * size), F32),
        pltpu.VMEM((rows, n * CAP * size), BF16),
        pltpu.VMEM((blocks, size, 6 * size), BF16),
        pltpu.VMEM((edges, size, 2 * size), BF16),
        pltpu.VMEM((4, half * 8, 2 * size), F32),
        pltpu.VMEM((half * stride, 2 * size), F32),
        pltpu.VMEM((feats, 5 * feats), F32),
        pltpu.VMEM((8, feats), F32),
        pltpu.VMEM((rows, feats), F32),
        pltpu.VMEM((rows, feats), F32),
        dma((2, n)),
        dma((2, n)),
        dma((n,)),
        dma((n,)),
        dma((2, 2, 2)),
        dma((2, 2, 2)),
    ]
    near_flops = 2 * 2 * 5 * rows * size * feats
    return pl.pallas_call(
        functools.partial(kernel, n, ny),
        out_shape=jax.ShapeDtypeStruct(cell_input.shape, BF16),
        in_specs=[vmem] * 6 + [smem] * 3 + [vmem] * 3,
        out_specs=vmem,
        scratch_shapes=scratch,
        cost_estimate=pl.CostEstimate(
            flops=near_flops, bytes_accessed=2 * rows * feats * 2, transcendentals=2 * rows * feats
        ),
        compiler_params=pltpu.CompilerParams(
            collective_id=0, has_side_effects=True, vmem_limit_bytes=40 * 1024 * 1024
        ),
    )(
        cell_input,
        w_filter,
        w_gate,
        bias_filter.reshape(1, channels),
        bias_gate.reshape(1, channels),
        adjacency,
        out_block,
        out_dev,
        out_target,
        out_tiles,
        w_mix,
        bias_mix.reshape(1, channels),
    )


def solution(mesh):
    in_specs = (
        P("rx", "ry", None, None),
        P(),
        P(),
        P(),
        P(),
        P("rx", "ry", None, None),
        P("rx", "ry", None),
        P("rx", "ry", None, None),
        P("rx", "ry", None),
        P("rx", "ry", None, None),
        P(),
        P(),
    )
    out_specs = P("rx", "ry", None, None)
    body = functools.partial(local, mesh.shape["rx"], mesh.shape["ry"])
    return jax.shard_map(body, mesh=mesh, in_specs=in_specs, out_specs=out_specs, check_vma=False)
```

```python
import functools

import jax
import jax.numpy as jnp
from jax import lax
from jax.experimental import pallas as pl
from jax.experimental.pallas import tpu as pltpu
from jax.sharding import PartitionSpec as P

DILATION_STEP = 2
CAP = 2
MESH = pl.DeviceIdType.MESH
F32 = jnp.float32
BF16 = jnp.bfloat16


def dot(a, b):
    return jnp.dot(a, b, preferred_element_type=F32)


def each(count, body, limit=8):
    if count <= limit:
        for k in range(count):
            body(k)
    else:

        def step(k, carry):
            body(k)
            return carry

        lax.fori_loop(0, count, step, 0)


def blocks_loop(count, body, unroll):
    def step(k, carry):
        body(k)
        return carry

    lax.fori_loop(0, count, step, 0, unroll=unroll)


def kernel(
    n,
    ny,
    *refs,
):
    inputs, (out, *landing), refs = refs[:12], refs[12:25], refs[25:]
    (
        cell,
        w_filter,
        w_gate,
        bias_filter,
        bias_gate,
        adjacency,
        out_block,
        out_dev,
        out_target,
        out_tiles,
        w_mix,
        bias_mix,
    ) = landing
    (
    gated,
    first,
    halo_rows,
    halo_cols,
    send_buf,
    recv_buf,
    target_send,
    target_recv,
    select,
    tiles,
    edge_tiles,
    spread,
    edge_spread,
    table,
    bias_table,
    acc,
    base,
    send_sem,
    recv_sem,
    target_send_sem,
    target_recv_sem,
    halo_send_sem,
    halo_recv_sem,
    fetch_sem,
    ) = refs
    fetches = [
        pltpu.make_async_copy(src, dst, fetch_sem.at[k])
        for k, (src, dst) in enumerate(zip(inputs, landing))
    ]
    for k in (1, 2, 3, 4, 9, 6, 7, 8, 0, 10, 11, 5):
        fetches[k].start()
    br, bc, size, feats = cell.shape
    blocks = br * bc
    rows = blocks * size
    half = size // 2
    edges = out_tiles.shape[2]
    channels = w_filter.shape[1]
    steps = feats // channels
    stride = edge_spread.shape[0] // half
    rx = lax.axis_index("rx")
    ry = lax.axis_index("ry")

    barrier = pltpu.get_barrier_semaphore()

    def greet(k):
        pl.semaphore_signal(
            barrier, inc=1, device_id={"rx": lax.rem(rx + k + 1, n)}, device_id_type=MESH
        )

    each(n - 1, greet)

    @pl.when(ry > 0)
    def _():
        pl.semaphore_signal(barrier, inc=1, device_id={"ry": ry - 1}, device_id_type=MESH)

    @pl.when(ry < ny - 1)
    def _():
        pl.semaphore_signal(barrier, inc=1, device_id={"ry": ry + 1}, device_id_type=MESH)

    zero_side = jnp.zeros((2,) + halo_rows.shape[2:], BF16)

    @pl.when(rx == 0)
    def _():
        halo_rows[:, 0] = zero_side

    @pl.when(rx == n - 1)
    def _():
        halo_rows[:, 1] = zero_side

    @pl.when(ry == 0)
    def _():
        halo_cols[:, 0] = zero_side

    @pl.when(ry == ny - 1)
    def _():
        halo_cols[:, 1] = zero_side

    for k in range(12):
        if k != 5:
            fetches[k].wait()

    table[...] = jnp.zeros_like(table)
    for t in range(steps):
        span = slice(t * channels, (t + 1) * channels)
        for which, weights in enumerate((w_filter, w_gate)):
            for tap, to in ((1, t), (0, t + DILATION_STEP)):
                if to < steps:
                    at = which * feats + to * channels
                    table[span, at : at + channels] = weights[tap].astype(F32)
        for hop in range(3):
            at = (2 + hop) * feats + t * channels
            table[span, at : at + channels] = w_mix[hop].astype(F32)
        bias_table[0:1, span] = bias_filter[...]
        bias_table[1:2, span] = bias_gate[...]
        bias_table[2:3, span] = bias_mix[...]
    taps = table[:, : 2 * feats].astype(BF16)
    mixes = [table[:, (2 + h) * feats : (3 + h) * feats].astype(BF16) for h in range(3)]

    def gate(block_rows):
        pre = dot(block_rows, taps)
        pre_f = pre[:, :feats] + bias_table[0:1]
        pre_g = pre[:, feats:] + bias_table[1:2]
        value = jnp.tanh(pre_f) * (0.5 * jnp.tanh(0.5 * pre_g) + 0.5)
        return value.astype(BF16)

    for r in range(half):
        piece = out_tiles[0, 0, :, r * 2 * size : (r + 1) * 2 * size]
        edge_spread[r * stride : r * stride + edges] = piece.astype(F32)
    for e in range(edges):
        pairs = edge_spread[pl.ds(e, half, stride=stride), :]
        edge_tiles[e, :half] = pairs.astype(BF16)
        edge_tiles[e, half:] = pltpu.roll(pairs, size, 1).astype(BF16)

    def slots(d):
        head, tail = jnp.int32(-1), jnp.int32(-1)
        for e in range(edges):
            hit = out_dev[0, 0, e] == d
            head = jnp.where(hit & (head < 0), e, head)
            tail = jnp.where(hit, e, tail)
        return ((jnp.maximum(head, 0), head >= 0), (jnp.maximum(tail, 0), tail != head))

    lane = lax.broadcasted_iota(jnp.int32, (8, CAP * size), 1)

    def halo_copies(signal, hop):
        sides = []
        for which, (axis, here, count, halo) in enumerate(
            (("rx", rx, n, halo_rows), ("ry", ry, ny, halo_cols))
        ):
            last = (br if which == 0 else bc) - 1
            for side, (edge, step) in enumerate(((last, 1), (0, -1))):
                src = signal.at[edge] if which == 0 else signal.at[:, edge]
                copy = pltpu.make_async_remote_copy(
                    src_ref=src,
                    dst_ref=halo.at[hop, side],
                    send_sem=halo_send_sem.at[hop, which, side],
                    recv_sem=halo_recv_sem.at[hop, which, side],
                    device_id={axis: jnp.clip(here + step, 0, count - 1)},
                    device_id_type=MESH,
                )
                sends = (here < count - 1) if step == 1 else (here > 0)
                gets = (here > 0) if step == 1 else (here < count - 1)
                sides.append((sends, gets, copy))
        return sides

    def far_copy(hop, d, source):
        return pltpu.make_async_remote_copy(
            src_ref=send_buf.at[hop, d],
            dst_ref=recv_buf.at[hop, source],
            send_sem=send_sem.at[hop, d],
            recv_sem=recv_sem.at[hop, source],
            device_id={"rx": d},
            device_id_type=MESH,
        )

    def target_copy(d, source):
        return pltpu.make_async_remote_copy(
            src_ref=target_send.at[d],
            dst_ref=target_recv.at[source],
            send_sem=target_send_sem.at[d],
            recv_sem=target_recv_sem.at[source],
            device_id={"rx": d},
            device_id_type=MESH,
        )

    part = n // 2

    def destination(k):
        side = (rx // part + 1 + k // part) % 2
        return side * part + (rx % part + k % part + 1) % part

    def send_far(signal, hop):
        def one(k):
            d = destination(k)
            picked, targets = [], []
            for index, valid in slots(d):
                b = out_block[0, 0, index]
                block = signal[lax.div(b, bc), lax.rem(b, bc)]
                picked.append((index, valid, block))
                targets.append(jnp.where(valid, out_target[0, 0, index], -1))
            if hop == 0:
                both = gate(jnp.concatenate([block for _, _, block in picked], axis=0))
                values = [both[c * size : (c + 1) * size] for c in range(CAP)]
            else:
                values = [block for _, _, block in picked]
            products = []
            for (index, valid, _), block in zip(picked, values):
                product = dot(edge_tiles[index][:, :size], block)
                products.append((product * jnp.where(valid, 1.0, 0.0)).astype(BF16))
            both = jnp.concatenate(products, axis=0)
            named = jnp.where(lane < size, targets[0], targets[1]).astype(F32)
            own = k == n - 1

            def keep():
                recv_buf[hop, rx] = both
                if hop == 0:
                    target_recv[rx] = named

            def send():
                send_buf[hop, d] = both
                far_copy(hop, d, rx).start()
                if hop == 0:
                    target_send[d] = named
                    target_copy(d, rx).start()

            if isinstance(own, bool):
                keep() if own else send()
            else:
                pl.when(own)(keep)
                pl.when(jnp.logical_not(own))(send)

        each(n, one)

    part_pairs = n // 4

    def add_far(hop, finish):
        strip = bc * size

        def wait_source(source):
            far_copy(hop, source, source).wait_recv()

        def one(q):
            side = (rx // part + q // part_pairs) % 2
            pair = side * part_pairs + (rx % part // 2 + q % part_pairs) % part_pairs
            if isinstance(q, int) and q == 0:
                wait_source(rx + 1 - 2 * (rx % 2))
            else:
                wait_source(2 * pair)
                wait_source(2 * pair + 1)
            landed = recv_buf[hop, pl.ds(2 * pair, 2)].reshape(2 * CAP * size, feats)
            for i in range(br):
                span = slice(i * strip, (i + 1) * strip)
                total = acc[span] + dot(select[pair, span], landed)
                if isinstance(q, int) and q == n // 2 - 1:
                    finish(i, total)
                else:
                    acc[span] = total

        one(0)
        each(n // 2 - 2, lambda q: one(q + 1))
        one(n // 2 - 1)

    def near(signal, hop):
        for i in range(br):
            for j in range(bc):
                up = signal[i - 1, j] if i > 0 else halo_rows[hop, 0, j]
                down = signal[i + 1, j] if i < br - 1 else halo_rows[hop, 1, j]
                left = signal[i, j - 1] if j > 0 else halo_cols[hop, 0, i]
                right = signal[i, j + 1] if j < bc - 1 else halo_cols[hop, 1, i]
                column = jnp.concatenate([signal[i, j], up, down, left, right], axis=0)
                total = dot(tiles[i * bc + j][:, : 5 * size], column)
                at = (i * bc + j) * size
                acc[pl.ds(at, half, stride=2), :] = total[:half]
                acc[pl.ds(at + 1, half, stride=2), :] = total[half:]

    pl.semaphore_wait(
        barrier,
        n - 1 + jnp.where(ry > 0, 1, 0) + jnp.where(ry < ny - 1, 1, 0),
    )

    def start_halo(signal, hop):
        for sends, gets, copy in halo_copies(signal, hop):
            pl.when(sends)(copy.start)

    def wait_halo(signal, hop):
        for sends, gets, copy in halo_copies(signal, hop):
            pl.when(gets)(copy.wait_recv)

    send_far(cell, 0)
    for i in range(br):
        gated[i] = gate(cell[i].reshape(bc * size, feats)).reshape(bc, size, feats)
    start_halo(gated, 0)

    low = lax.broadcasted_iota(jnp.int32, (half, 2 * size), 1) < size

    def arrange(i):
        slot = lax.rem(i, spread.shape[0])
        for k in range(5):
            for r in range(half):
                piece = adjacency[i, k, :, r * 2 * size : (r + 1) * 2 * size]
                at = r * 8 + k % 2 * bc
                spread[slot, k // 2, at : at + bc] = piece.astype(F32)
        for j in range(bc):
            pairs = [
                spread[slot, k // 2, pl.ds(k % 2 * bc + j, half, stride=8), :] for k in range(5)
            ]
            turned = [pltpu.roll(pair, size, 1) for pair in pairs]
            zero = jnp.zeros_like(pairs[0])
            pairs.append(zero)
            turned.append(zero)
            for k in range(0, 6, 2):
                span = slice(k * size, (k + 2) * size)
                even = jnp.where(low, pairs[k], turned[k + 1])
                odd = jnp.where(low, turned[k], pairs[k + 1])
                tiles[i * bc + j, :half, span] = even.astype(BF16)
                tiles[i * bc + j, half:, span] = odd.astype(BF16)

    fetches[5].wait()
    blocks_loop(br, arrange, 2)

    wait_halo(gated, 0)
    near(gated, 0)

    def wait_target(k):
        source = lax.rem(rx + n - k - 1, n)
        target_copy(source, source).wait_recv()

    each(n - 1, wait_target)
    spot = lax.broadcasted_iota(jnp.int32, (size, CAP * size), 1) % size
    row = lax.broadcasted_iota(jnp.int32, (size, CAP * size), 0)
    unit = jnp.where(row == 2 * (spot % half) + spot // half, 1.0, 0.0).astype(BF16)
    for source in range(n):
        named = target_recv[source, 0:1]
        span = slice(source % 2 * CAP * size, (source % 2 + 1) * CAP * size)
        for block in range(blocks):
            hit = jnp.where(named == float(block), 1.0, 0.0).astype(BF16)
            select[source // 2, block * size : (block + 1) * size, span] = unit * hit

    strip = bc * size

    def end_first(i, total):
        first[i] = total.astype(BF16).reshape(bc, size, feats)

    add_far(0, end_first)
    send_far(first, 1)
    start_halo(first, 1)

    for i in range(br):
        own = dot(gated[i].reshape(strip, feats), mixes[0])
        own = own + dot(first[i].reshape(strip, feats), mixes[1]) + bias_table[2:3]
        base[i * strip : (i + 1) * strip] = own + cell[i].reshape(strip, feats).astype(F32)
    wait_halo(first, 1)
    near(first, 1)

    def end_second(i, second):
        upper = second.astype(BF16)
        lower = (second - upper.astype(F32)).astype(BF16)
        total = base[i * strip : (i + 1) * strip]
        total = total + (dot(upper, mixes[2]) + dot(lower, mixes[2]))
        out[i] = total.astype(BF16).reshape(bc, size, feats)

    add_far(1, end_second)

    for hop, signal in enumerate((gated, first)):
        for sends, gets, copy in halo_copies(signal, hop):
            pl.when(sends)(copy.wait_send)

        def sent(k):
            d = destination(k)
            far_copy(hop, d, rx).wait_send()
            if hop == 0:
                target_copy(d, rx).wait_send()

        each(n - 1, sent)


def local(
    n,
    ny,
    cell_input,
    w_filter,
    w_gate,
    bias_filter,
    bias_gate,
    adjacency,
    out_block,
    out_dev,
    out_target,
    out_tiles,
    w_mix,
    bias_mix,
):
    br, bc, size, feats = cell_input.shape
    blocks = br * bc
    rows = blocks * size
    edges = out_tiles.shape[2]
    channels = w_filter.shape[1]
    half = size // 2
    stride = -(-edges // 8) * 8
    assert feats == 128 and size == 64 and br == bc == 4 and n % 4 == 0
    vmem = pl.BlockSpec(memory_space=pltpu.VMEM)
    dma = pltpu.SemaphoreType.DMA
    hbm = pl.BlockSpec(memory_space=pltpu.HBM)
    operands = (
        cell_input,
        w_filter,
        w_gate,
        bias_filter.reshape(1, channels),
        bias_gate.reshape(1, channels),
        adjacency.transpose(0, 2, 1, 3),
        out_block,
        out_dev.reshape(out_block.shape),
        out_target,
        out_tiles,
        w_mix,
        bias_mix.reshape(1, channels),
    )
    scratch = [
        (pltpu.SMEM if k in (6, 7, 8) else pltpu.VMEM)(a.shape, a.dtype)
        for k, a in enumerate(operands)
    ] + [
        pltpu.VMEM((br, bc, size, feats), BF16),
        pltpu.VMEM((br, bc, size, feats), BF16),
        pltpu.VMEM((2, 2, bc, size, feats), BF16),
        pltpu.VMEM((2, 2, br, size, feats), BF16),
        pltpu.VMEM((2, n, CAP * size, feats), BF16),
        pltpu.VMEM((2, n, CAP * size, feats), BF16),
        pltpu.VMEM((n, 8, CAP * size), F32),
        pltpu.VMEM((n, 8, CAP * size), F32),
        pltpu.VMEM((n // 2, rows, 2 * CAP * size), BF16),
        pltpu.VMEM((blocks, size, 6 * size), BF16),
        pltpu.VMEM((edges, size, 2 * size), BF16),
        pltpu.VMEM((2, 3, half * 8, 2 * size), F32),
        pltpu.VMEM((half * stride, 2 * size), F32),
        pltpu.VMEM((feats, 5 * feats), F32),
        pltpu.VMEM((8, feats), F32),
        pltpu.VMEM((rows, feats), F32),
        pltpu.VMEM((rows, feats), F32),
        dma((2, n)),
        dma((2, n)),
        dma((n,)),
        dma((n,)),
        dma((2, 2, 2)),
        dma((2, 2, 2)),
        dma((12,)),
    ]
    near_flops = 2 * 2 * 5 * rows * size * feats
    return pl.pallas_call(
        functools.partial(kernel, n, ny),
        out_shape=jax.ShapeDtypeStruct(cell_input.shape, BF16),
        in_specs=[hbm] * 12,
        out_specs=vmem,
        scratch_shapes=scratch,
        cost_estimate=pl.CostEstimate(
            flops=near_flops, bytes_accessed=2 * rows * feats * 2, transcendentals=2 * rows * feats
        ),
        compiler_params=pltpu.CompilerParams(
            collective_id=0, has_side_effects=True, vmem_limit_bytes=63 * 1024 * 1024
        ),
    )(*operands)


def solution(mesh):
    in_specs = (
        P("rx", "ry", None, None),
        P(),
        P(),
        P(),
        P(),
        P("rx", "ry", None, None),
        P("rx", "ry", None),
        P("rx", "ry", None, None),
        P("rx", "ry", None),
        P("rx", "ry", None, None),
        P(),
        P(),
    )
    out_specs = P("rx", "ry", None, None)
    body = functools.partial(local, mesh.shape["rx"], mesh.shape["ry"])
    return jax.shard_map(body, mesh=mesh, in_specs=in_specs, out_specs=out_specs, check_vma=False)
```

```python
import functools

import jax
import jax.numpy as jnp
from jax import lax
from jax.experimental import pallas as pl
from jax.experimental.pallas import tpu as pltpu
from jax.sharding import PartitionSpec as P

DILATION_STEP = 2
CAP = 2
MESH = pl.DeviceIdType.MESH
F32 = jnp.float32
BF16 = jnp.bfloat16


def dot(a, b):
    return jnp.dot(a, b, preferred_element_type=F32)


def each(count, body, limit=8):
    if count <= limit:
        for k in range(count):
            body(k)
    else:

        def step(k, carry):
            body(k)
            return carry

        lax.fori_loop(0, count, step, 0)


def blocks_loop(count, body, unroll):
    def step(k, carry):
        body(k)
        return carry

    lax.fori_loop(0, count, step, 0, unroll=unroll)


def kernel(
    n,
    ny,
    *refs,
):
    inputs, (out, *landing), refs = refs[:12], refs[12:25], refs[25:]
    (
        cell,
        w_filter,
        w_gate,
        bias_filter,
        bias_gate,
        adjacency,
        out_block,
        out_dev,
        out_target,
        out_tiles,
        w_mix,
        bias_mix,
    ) = landing
    (
    gated,
    first,
    halo_rows,
    halo_cols,
    send_buf,
    recv_buf,
    target_send,
    target_recv,
    select,
    tiles,
    edge_tiles,
    spread,
    edge_spread,
    table,
    bias_table,
    acc,
    base,
    send_sem,
    recv_sem,
    target_send_sem,
    target_recv_sem,
    halo_send_sem,
    halo_recv_sem,
    fetch_sem,
    route,
    ) = refs
    fetches = [
        pltpu.make_async_copy(src, dst, fetch_sem.at[k])
        for k, (src, dst) in enumerate(zip(inputs, landing))
    ]
    for k in (1, 2, 3, 4, 9, 6, 7, 8, 0, 10, 11, 5):
        fetches[k].start()
    br, bc, size, feats = cell.shape
    blocks = br * bc
    rows = blocks * size
    half = size // 2
    edges = out_tiles.shape[2]
    channels = w_filter.shape[1]
    steps = feats // channels
    stride = edge_spread.shape[0] // half
    rx = lax.axis_index("rx")
    ry = lax.axis_index("ry")

    barrier = pltpu.get_barrier_semaphore()

    def greet(k):
        pl.semaphore_signal(
            barrier, inc=1, device_id={"rx": lax.rem(rx + k + 1, n)}, device_id_type=MESH
        )

    each(n - 1, greet)

    @pl.when(ry > 0)
    def _():
        pl.semaphore_signal(barrier, inc=1, device_id={"ry": ry - 1}, device_id_type=MESH)

    @pl.when(ry < ny - 1)
    def _():
        pl.semaphore_signal(barrier, inc=1, device_id={"ry": ry + 1}, device_id_type=MESH)

    zero_side = jnp.zeros((2,) + halo_rows.shape[2:], BF16)

    @pl.when(rx == 0)
    def _():
        halo_rows[:, 0] = zero_side

    @pl.when(rx == n - 1)
    def _():
        halo_rows[:, 1] = zero_side

    @pl.when(ry == 0)
    def _():
        halo_cols[:, 0] = zero_side

    @pl.when(ry == ny - 1)
    def _():
        halo_cols[:, 1] = zero_side

    for k in range(12):
        if k not in (0, 5):
            fetches[k].wait()

    table[...] = jnp.zeros_like(table)
    for t in range(steps):
        span = slice(t * channels, (t + 1) * channels)
        for which, weights in enumerate((w_filter, w_gate)):
            for tap, to in ((1, t), (0, t + DILATION_STEP)):
                if to < steps:
                    at = which * feats + to * channels
                    table[span, at : at + channels] = weights[tap].astype(F32)
        for hop in range(3):
            at = (2 + hop) * feats + t * channels
            table[span, at : at + channels] = w_mix[hop].astype(F32)
        bias_table[0:1, span] = bias_filter[...]
        bias_table[1:2, span] = bias_gate[...]
        bias_table[2:3, span] = bias_mix[...]
    taps = table[:, : 2 * feats].astype(BF16)
    mixes = [table[:, (2 + h) * feats : (3 + h) * feats].astype(BF16) for h in range(3)]
    early_mix = jnp.concatenate(mixes[:2], axis=0)
    late_mix = jnp.concatenate([mixes[2], mixes[2]], axis=0)

    def gate(block_rows):
        pre = dot(block_rows, taps)
        pre_f = pre[:, :feats] + bias_table[0:1]
        pre_g = pre[:, feats:] + bias_table[1:2]
        value = jnp.tanh(pre_f) * (0.5 * jnp.tanh(0.5 * pre_g) + 0.5)
        return value.astype(BF16)

    for r in range(half):
        piece = out_tiles[0, 0, :, r * 2 * size : (r + 1) * 2 * size]
        edge_spread[r * stride : r * stride + edges] = piece.astype(F32)
    for e in range(edges):
        pairs = edge_spread[pl.ds(e, half, stride=stride), :]
        edge_tiles[e, :half] = pairs.astype(BF16)
        edge_tiles[e, half:] = pltpu.roll(pairs, size, 1).astype(BF16)

    part = n // 2

    def destination(k):
        side = (rx // part + 1 + k // part) % 2
        return side * part + (rx % part + k % part + 1) % part

    lane = lax.broadcasted_iota(jnp.int32, (8, CAP * size), 1)

    def halo_copies(signal, hop):
        sides = []
        for which, (axis, here, count, halo) in enumerate(
            (("rx", rx, n, halo_rows), ("ry", ry, ny, halo_cols))
        ):
            last = (br if which == 0 else bc) - 1
            for side, (edge, step) in enumerate(((last, 1), (0, -1))):
                src = signal.at[edge] if which == 0 else signal.at[:, edge]
                copy = pltpu.make_async_remote_copy(
                    src_ref=src,
                    dst_ref=halo.at[hop, side],
                    send_sem=halo_send_sem.at[hop, which, side],
                    recv_sem=halo_recv_sem.at[hop, which, side],
                    device_id={axis: jnp.clip(here + step, 0, count - 1)},
                    device_id_type=MESH,
                )
                sends = (here < count - 1) if step == 1 else (here > 0)
                gets = (here > 0) if step == 1 else (here < count - 1)
                sides.append((sends, gets, copy))
        return sides

    def far_copy(hop, d, source):
        return pltpu.make_async_remote_copy(
            src_ref=send_buf.at[hop, d],
            dst_ref=recv_buf.at[hop, source],
            send_sem=send_sem.at[hop, d],
            recv_sem=recv_sem.at[hop, source],
            device_id={"rx": d},
            device_id_type=MESH,
        )

    def target_copy(d, source):
        return pltpu.make_async_remote_copy(
            src_ref=target_send.at[d],
            dst_ref=target_recv.at[source],
            send_sem=target_send_sem.at[d],
            recv_sem=target_recv_sem.at[source],
            device_id={"rx": d},
            device_id_type=MESH,
        )

    def find_route(k):
        d = destination(k)
        head, tail = jnp.int32(-1), jnp.int32(-1)
        for e in range(edges):
            hit = out_dev[0, 0, e] == d
            head = jnp.where(hit & (head < 0), e, head)
            tail = jnp.where(hit, e, tail)
        found = ((head, head >= 0), (tail, tail != head))
        for c, (index, valid) in enumerate(found):
            index = jnp.maximum(index, 0)
            route[k, c] = index
            route[k, CAP + c] = out_block[0, 0, index]
            route[k, 2 * CAP + c] = jnp.where(valid, 1, 0)

    def send_targets(k, own):
        d = destination(k)
        names = [
            jnp.where(route[k, 2 * CAP + c] == 1, out_target[0, 0, route[k, c]], -1)
            for c in range(CAP)
        ]
        named = jnp.where(lane < size, names[0], names[1]).astype(F32)
        if own:
            target_recv[rx] = named
        else:
            target_send[d] = named
            target_copy(d, rx).start()

    team = 4

    def send_group(signal, hop, start, last, gating):
        ks = [start + g for g in range(team)]
        picked = []
        for k in ks:
            for c in range(CAP):
                b = route[k, CAP + c]
                picked.append(signal[lax.div(b, bc), lax.rem(b, bc)])
        if gating:
            gates = gate(jnp.concatenate(picked, axis=0))
            picked = [gates[p * size : (p + 1) * size] for p in range(team * CAP)]
        sums = []
        for g, k in enumerate(ks):
            for c in range(CAP):
                product = dot(edge_tiles[route[k, c]][:, :size], picked[g * CAP + c])
                sums.append((product * route[k, 2 * CAP + c].astype(F32)).astype(BF16))
        for g, k in enumerate(ks):
            both = jnp.concatenate(sums[g * CAP : (g + 1) * CAP], axis=0)
            if last and g == team - 1:
                recv_buf[hop, rx] = both
            else:
                send_buf[hop, destination(k)] = both
        for g, k in enumerate(ks):
            if not (last and g == team - 1):
                far_copy(hop, destination(k), rx).start()

    def send_rest(signal, hop):
        each(n // team - 2, lambda g: send_group(signal, hop, (g + 1) * team, False, False))
        send_group(signal, hop, n - team, True, False)

    part_pairs = n // 4

    def add_far(hop, finish):
        strip = bc * size

        def wait_source(source):
            far_copy(hop, source, source).wait_recv()

        def one(q):
            side = (rx // part + q // part_pairs) % 2
            pair = side * part_pairs + (rx % part // 2 + q % part_pairs) % part_pairs
            if isinstance(q, int) and q == 0:
                wait_source(rx + 1 - 2 * (rx % 2))
            else:
                wait_source(2 * pair)
                wait_source(2 * pair + 1)
            landed = recv_buf[hop, pl.ds(2 * pair, 2)].reshape(2 * CAP * size, feats)
            for i in range(br):
                span = slice(i * strip, (i + 1) * strip)
                total = acc[span] + dot(select[pair, span], landed)
                if isinstance(q, int) and q == n // 2 - 1:
                    finish(i, total)
                else:
                    acc[span] = total

        one(0)
        each(n // 2 - 2, lambda q: one(q + 1))
        one(n // 2 - 1)

    def near(signal, hop):
        for i in range(br):
            for j in range(bc):
                up = signal[i - 1, j] if i > 0 else halo_rows[hop, 0, j]
                down = signal[i + 1, j] if i < br - 1 else halo_rows[hop, 1, j]
                left = signal[i, j - 1] if j > 0 else halo_cols[hop, 0, i]
                right = signal[i, j + 1] if j < bc - 1 else halo_cols[hop, 1, i]
                column = jnp.concatenate([signal[i, j], up, down, left, right], axis=0)
                total = dot(tiles[i * bc + j][:, : 5 * size], column)
                at = (i * bc + j) * size
                acc[pl.ds(at, half, stride=2), :] = total[:half]
                acc[pl.ds(at + 1, half, stride=2), :] = total[half:]

    each(n, find_route)
    pl.semaphore_wait(
        barrier,
        n - 1 + jnp.where(ry > 0, 1, 0) + jnp.where(ry < ny - 1, 1, 0),
    )

    def start_halo(signal, hop):
        for sends, gets, copy in halo_copies(signal, hop):
            pl.when(sends)(copy.start)

    def wait_halo(signal, hop):
        for sends, gets, copy in halo_copies(signal, hop):
            pl.when(gets)(copy.wait_recv)

    each(n - 1, lambda k: send_targets(k, False))
    send_targets(n - 1, True)
    fetches[0].wait()
    send_group(cell, 0, 0, False, True)
    for i in range(br):
        gated[i] = gate(cell[i].reshape(bc * size, feats)).reshape(bc, size, feats)
    start_halo(gated, 0)
    send_rest(gated, 0)

    low = lax.broadcasted_iota(jnp.int32, (half, 2 * size), 1) < size

    def arrange(i):
        slot = lax.rem(i, spread.shape[0])
        for k in range(5):
            for r in range(half):
                piece = adjacency[i, k, :, r * 2 * size : (r + 1) * 2 * size]
                at = r * 8 + k % 2 * bc
                spread[slot, k // 2, at : at + bc] = piece.astype(F32)
        for j in range(bc):
            pairs = [
                spread[slot, k // 2, pl.ds(k % 2 * bc + j, half, stride=8), :] for k in range(5)
            ]
            turned = [pltpu.roll(pair, size, 1) for pair in pairs]
            zero = jnp.zeros_like(pairs[0])
            pairs.append(zero)
            turned.append(zero)
            for k in range(0, 6, 2):
                span = slice(k * size, (k + 2) * size)
                even = jnp.where(low, pairs[k], turned[k + 1])
                odd = jnp.where(low, turned[k], pairs[k + 1])
                tiles[i * bc + j, :half, span] = even.astype(BF16)
                tiles[i * bc + j, half:, span] = odd.astype(BF16)

    fetches[5].wait()
    blocks_loop(br, arrange, 2)

    wait_halo(gated, 0)
    near(gated, 0)

    def wait_target(k):
        source = lax.rem(rx + n - k - 1, n)
        target_copy(source, source).wait_recv()

    each(n - 1, wait_target)
    spot = lax.broadcasted_iota(jnp.int32, (size, CAP * size), 1) % size
    row = lax.broadcasted_iota(jnp.int32, (size, CAP * size), 0)
    unit = jnp.where(row == 2 * (spot % half) + spot // half, 1.0, 0.0).astype(BF16)
    for source in range(n):
        named = target_recv[source, 0:1]
        span = slice(source % 2 * CAP * size, (source % 2 + 1) * CAP * size)
        for block in range(blocks):
            hit = jnp.where(named == float(block), 1.0, 0.0).astype(BF16)
            select[source // 2, block * size : (block + 1) * size, span] = unit * hit

    strip = bc * size

    def end_first(i, total):
        first[i] = total.astype(BF16).reshape(bc, size, feats)

    add_far(0, end_first)
    send_group(first, 1, 0, False, False)
    start_halo(first, 1)
    send_rest(first, 1)

    for i in range(br):
        known = [gated[i].reshape(strip, feats), first[i].reshape(strip, feats)]
        own = dot(jnp.concatenate(known, axis=1), early_mix) + bias_table[2:3]
        base[i * strip : (i + 1) * strip] = own + cell[i].reshape(strip, feats).astype(F32)
    wait_halo(first, 1)
    near(first, 1)

    def end_second(i, second):
        upper = second.astype(BF16)
        lower = (second - upper.astype(F32)).astype(BF16)
        total = base[i * strip : (i + 1) * strip]
        total = total + dot(jnp.concatenate([upper, lower], axis=1), late_mix)
        out[i] = total.astype(BF16).reshape(bc, size, feats)

    add_far(1, end_second)

    for hop, signal in enumerate((gated, first)):
        for sends, gets, copy in halo_copies(signal, hop):
            pl.when(sends)(copy.wait_send)

        def sent(k):
            d = destination(k)
            far_copy(hop, d, rx).wait_send()
            if hop == 0:
                target_copy(d, rx).wait_send()

        each(n - 1, sent)


def local(
    n,
    ny,
    cell_input,
    w_filter,
    w_gate,
    bias_filter,
    bias_gate,
    adjacency,
    out_block,
    out_dev,
    out_target,
    out_tiles,
    w_mix,
    bias_mix,
):
    br, bc, size, feats = cell_input.shape
    blocks = br * bc
    rows = blocks * size
    edges = out_tiles.shape[2]
    channels = w_filter.shape[1]
    half = size // 2
    stride = -(-edges // 8) * 8
    assert feats == 128 and size == 64 and br == bc == 4 and n % 4 == 0
    vmem = pl.BlockSpec(memory_space=pltpu.VMEM)
    dma = pltpu.SemaphoreType.DMA
    hbm = pl.BlockSpec(memory_space=pltpu.HBM)
    operands = (
        cell_input,
        w_filter,
        w_gate,
        bias_filter.reshape(1, channels),
        bias_gate.reshape(1, channels),
        adjacency.transpose(0, 2, 1, 3),
        out_block,
        out_dev.reshape(out_block.shape),
        out_target,
        out_tiles,
        w_mix,
        bias_mix.reshape(1, channels),
    )
    scratch = [
        (pltpu.SMEM if k in (6, 7, 8) else pltpu.VMEM)(a.shape, a.dtype)
        for k, a in enumerate(operands)
    ] + [
        pltpu.VMEM((br, bc, size, feats), BF16),
        pltpu.VMEM((br, bc, size, feats), BF16),
        pltpu.VMEM((2, 2, bc, size, feats), BF16),
        pltpu.VMEM((2, 2, br, size, feats), BF16),
        pltpu.VMEM((2, n, CAP * size, feats), BF16),
        pltpu.VMEM((2, n, CAP * size, feats), BF16),
        pltpu.VMEM((n, 8, CAP * size), F32),
        pltpu.VMEM((n, 8, CAP * size), F32),
        pltpu.VMEM((n // 2, rows, 2 * CAP * size), BF16),
        pltpu.VMEM((blocks, size, 6 * size), BF16),
        pltpu.VMEM((edges, size, 2 * size), BF16),
        pltpu.VMEM((2, 3, half * 8, 2 * size), F32),
        pltpu.VMEM((half * stride, 2 * size), F32),
        pltpu.VMEM((feats, 5 * feats), F32),
        pltpu.VMEM((8, feats), F32),
        pltpu.VMEM((rows, feats), F32),
        pltpu.VMEM((rows, feats), F32),
        dma((2, n)),
        dma((2, n)),
        dma((n,)),
        dma((n,)),
        dma((2, 2, 2)),
        dma((2, 2, 2)),
        dma((12,)),
        pltpu.SMEM((n, 3 * CAP), jnp.int32),
    ]
    near_flops = 2 * 2 * 5 * rows * size * feats
    return pl.pallas_call(
        functools.partial(kernel, n, ny),
        out_shape=jax.ShapeDtypeStruct(cell_input.shape, BF16),
        in_specs=[hbm] * 12,
        out_specs=vmem,
        scratch_shapes=scratch,
        cost_estimate=pl.CostEstimate(
            flops=near_flops, bytes_accessed=2 * rows * feats * 2, transcendentals=2 * rows * feats
        ),
        compiler_params=pltpu.CompilerParams(
            collective_id=0, has_side_effects=True, vmem_limit_bytes=40 * 1024 * 1024
        ),
    )(*(pltpu.with_memory_space_constraint(a, pltpu.HBM) for a in operands))


def solution(mesh):
    in_specs = (
        P("rx", "ry", None, None),
        P(),
        P(),
        P(),
        P(),
        P("rx", "ry", None, None),
        P("rx", "ry", None),
        P("rx", "ry", None, None),
        P("rx", "ry", None),
        P("rx", "ry", None, None),
        P(),
        P(),
    )
    out_specs = P("rx", "ry", None, None)
    body = functools.partial(local, mesh.shape["rx"], mesh.shape["ry"])
    return jax.shard_map(body, mesh=mesh, in_specs=in_specs, out_specs=out_specs, check_vma=False)
```

```python
import functools

import jax
import jax.numpy as jnp
from jax import lax
from jax.experimental import pallas as pl
from jax.experimental.pallas import tpu as pltpu
from jax.sharding import PartitionSpec as P

DILATION_STEP = 2
CAP = 2
MESH = pl.DeviceIdType.MESH
F32 = jnp.float32
BF16 = jnp.bfloat16


def dot(a, b):
    return jnp.dot(a, b, preferred_element_type=F32)


def each(count, body, limit=8):
    if count <= limit:
        for k in range(count):
            body(k)
    else:

        def step(k, carry):
            body(k)
            return carry

        lax.fori_loop(0, count, step, 0)


def blocks_loop(count, body, unroll):
    def step(k, carry):
        body(k)
        return carry

    lax.fori_loop(0, count, step, 0, unroll=unroll)


def kernel(
    n,
    ny,
    *refs,
):
    inputs, (out, *landing), refs = refs[:12], refs[12:25], refs[25:]
    (
        cell,
        w_filter,
        w_gate,
        bias_filter,
        bias_gate,
        adjacency,
        out_block,
        out_dev,
        out_target,
        out_tiles,
        w_mix,
        bias_mix,
    ) = landing
    (
    gated,
    first,
    halo_rows,
    halo_cols,
    send_buf,
    recv_buf,
    target_send,
    target_recv,
    select,
    tiles,
    edge_tiles,
    spread,
    edge_spread,
    table,
    bias_table,
    acc,
    base,
    send_sem,
    recv_sem,
    target_send_sem,
    target_recv_sem,
    halo_send_sem,
    halo_recv_sem,
    fetch_sem,
    route,
    ) = refs
    fetches = [
        pltpu.make_async_copy(src, dst, fetch_sem.at[k])
        for k, (src, dst) in enumerate(zip(inputs, landing))
    ]
    for k in (1, 2, 3, 4, 9, 6, 7, 8, 0, 10, 11, 5):
        fetches[k].start()
    br, bc, size, feats = cell.shape
    blocks = br * bc
    rows = blocks * size
    half = size // 2
    edges = out_tiles.shape[2]
    channels = w_filter.shape[1]
    steps = feats // channels
    stride = edge_spread.shape[0] // half
    rx = lax.axis_index("rx")
    ry = lax.axis_index("ry")

    barrier = pltpu.get_barrier_semaphore()

    def greet(k):
        pl.semaphore_signal(
            barrier, inc=1, device_id={"rx": lax.rem(rx + k + 1, n)}, device_id_type=MESH
        )

    each(n - 1, greet)

    @pl.when(ry > 0)
    def _():
        pl.semaphore_signal(barrier, inc=1, device_id={"ry": ry - 1}, device_id_type=MESH)

    @pl.when(ry < ny - 1)
    def _():
        pl.semaphore_signal(barrier, inc=1, device_id={"ry": ry + 1}, device_id_type=MESH)

    zero_side = jnp.zeros((2,) + halo_rows.shape[2:], BF16)

    @pl.when(rx == 0)
    def _():
        halo_rows[:, 0] = zero_side

    @pl.when(rx == n - 1)
    def _():
        halo_rows[:, 1] = zero_side

    @pl.when(ry == 0)
    def _():
        halo_cols[:, 0] = zero_side

    @pl.when(ry == ny - 1)
    def _():
        halo_cols[:, 1] = zero_side

    for k in range(12):
        if k not in (0, 5):
            fetches[k].wait()

    table[...] = jnp.zeros_like(table)
    for t in range(steps):
        span = slice(t * channels, (t + 1) * channels)
        for which, weights in enumerate((w_filter, w_gate)):
            for tap, to in ((1, t), (0, t + DILATION_STEP)):
                if to < steps:
                    at = which * feats + to * channels
                    table[span, at : at + channels] = weights[tap].astype(F32)
        for hop in range(3):
            at = (2 + hop) * feats + t * channels
            table[span, at : at + channels] = w_mix[hop].astype(F32)
        bias_table[0:1, span] = bias_filter[...]
        bias_table[1:2, span] = bias_gate[...]
        bias_table[2:3, span] = bias_mix[...]
    taps = table[:, : 2 * feats].astype(BF16)
    mixes = [table[:, (2 + h) * feats : (3 + h) * feats].astype(BF16) for h in range(3)]
    early_mix = jnp.concatenate(mixes[:2], axis=0)
    late_mix = jnp.concatenate([mixes[2], mixes[2]], axis=0)

    def gate(block_rows):
        pre = dot(block_rows, taps)
        pre_f = pre[:, :feats] + bias_table[0:1]
        pre_g = pre[:, feats:] + bias_table[1:2]
        value = jnp.tanh(pre_f) * (0.5 * jnp.tanh(0.5 * pre_g) + 0.5)
        return value.astype(BF16)

    for r in range(half):
        piece = out_tiles[0, 0, :, r * 2 * size : (r + 1) * 2 * size]
        edge_spread[r * stride : r * stride + edges] = piece.astype(F32)
    for e in range(edges):
        pairs = edge_spread[pl.ds(e, half, stride=stride), :]
        edge_tiles[e, :half] = pairs.astype(BF16)
        edge_tiles[e, half:] = pltpu.roll(pairs, size, 1).astype(BF16)

    part = n // 2

    def destination(k):
        side = (rx // part + 1 + k // part) % 2
        return side * part + (rx % part + k % part + 1) % part

    lane = lax.broadcasted_iota(jnp.int32, (8, CAP * size), 1)

    def halo_copies(signal, hop):
        sides = []
        for which, (axis, here, count, halo) in enumerate(
            (("rx", rx, n, halo_rows), ("ry", ry, ny, halo_cols))
        ):
            last = (br if which == 0 else bc) - 1
            for side, (edge, step) in enumerate(((last, 1), (0, -1))):
                src = signal.at[edge] if which == 0 else signal.at[:, edge]
                copy = pltpu.make_async_remote_copy(
                    src_ref=src,
                    dst_ref=halo.at[hop, side],
                    send_sem=halo_send_sem.at[hop, which, side],
                    recv_sem=halo_recv_sem.at[hop, which, side],
                    device_id={axis: jnp.clip(here + step, 0, count - 1)},
                    device_id_type=MESH,
                )
                sends = (here < count - 1) if step == 1 else (here > 0)
                gets = (here > 0) if step == 1 else (here < count - 1)
                sides.append((sends, gets, copy))
        return sides

    def far_copy(hop, d, source):
        return pltpu.make_async_remote_copy(
            src_ref=send_buf.at[hop, d],
            dst_ref=recv_buf.at[hop, source],
            send_sem=send_sem.at[hop, d],
            recv_sem=recv_sem.at[hop, source],
            device_id={"rx": d},
            device_id_type=MESH,
        )

    def target_copy(d, source):
        return pltpu.make_async_remote_copy(
            src_ref=target_send.at[d],
            dst_ref=target_recv.at[source],
            send_sem=target_send_sem.at[d],
            recv_sem=target_recv_sem.at[source],
            device_id={"rx": d},
            device_id_type=MESH,
        )

    def find_route(k):
        d = destination(k)
        head, tail = jnp.int32(-1), jnp.int32(-1)
        for e in range(edges):
            hit = out_dev[0, 0, e] == d
            head = jnp.where(hit & (head < 0), e, head)
            tail = jnp.where(hit, e, tail)
        found = ((head, head >= 0), (tail, tail != head))
        for c, (index, valid) in enumerate(found):
            index = jnp.maximum(index, 0)
            route[k, c] = index
            route[k, CAP + c] = out_block[0, 0, index]
            route[k, 2 * CAP + c] = jnp.where(valid, 1, 0)

    def send_targets(k, own):
        d = destination(k)
        names = [
            jnp.where(route[k, 2 * CAP + c] == 1, out_target[0, 0, route[k, c]], -1)
            for c in range(CAP)
        ]
        named = jnp.where(lane < size, names[0], names[1]).astype(F32)
        if own:
            target_recv[rx] = named
        else:
            target_send[d] = named
            target_copy(d, rx).start()

    team = 4

    def send_group(signal, hop, start, last):
        ks = [start + g for g in range(team)]
        picked = []
        for k in ks:
            for c in range(CAP):
                b = route[k, CAP + c]
                picked.append(signal[lax.div(b, bc), lax.rem(b, bc)])
        sums = []
        for g, k in enumerate(ks):
            for c in range(CAP):
                product = dot(edge_tiles[route[k, c]][:, :size], picked[g * CAP + c])
                sums.append((product * route[k, 2 * CAP + c].astype(F32)).astype(BF16))
        for g, k in enumerate(ks):
            both = jnp.concatenate(sums[g * CAP : (g + 1) * CAP], axis=0)
            if last and g == team - 1:
                recv_buf[hop, rx] = both
            else:
                send_buf[hop, destination(k)] = both
        for g, k in enumerate(ks):
            if not (last and g == team - 1):
                far_copy(hop, destination(k), rx).start()

    def send_far(signal, hop):
        each(n // team - 1, lambda g: send_group(signal, hop, g * team, False))
        send_group(signal, hop, n - team, True)

    part_pairs = n // 4

    def add_far(hop, finish):
        strip = bc * size

        def wait_source(source):
            far_copy(hop, source, source).wait_recv()

        def one(q):
            side = (rx // part + q // part_pairs) % 2
            pair = side * part_pairs + (rx % part // 2 + q % part_pairs) % part_pairs
            if isinstance(q, int) and q == 0:
                wait_source(rx + 1 - 2 * (rx % 2))
            else:
                wait_source(2 * pair)
                wait_source(2 * pair + 1)
            landed = recv_buf[hop, pl.ds(2 * pair, 2)].reshape(2 * CAP * size, feats)
            for i in range(br):
                span = slice(i * strip, (i + 1) * strip)
                total = acc[span] + dot(select[pair, span], landed)
                if isinstance(q, int) and q == n // 2 - 1:
                    finish(i, total)
                else:
                    acc[span] = total

        one(0)
        each(n // 2 - 2, lambda q: one(q + 1))
        one(n // 2 - 1)

    def near(signal, hop):
        for i in range(br):
            for j in range(bc):
                up = signal[i - 1, j] if i > 0 else halo_rows[hop, 0, j]
                down = signal[i + 1, j] if i < br - 1 else halo_rows[hop, 1, j]
                left = signal[i, j - 1] if j > 0 else halo_cols[hop, 0, i]
                right = signal[i, j + 1] if j < bc - 1 else halo_cols[hop, 1, i]
                column = jnp.concatenate([signal[i, j], up, down, left, right], axis=0)
                total = dot(tiles[i * bc + j][:, : 5 * size], column)
                at = (i * bc + j) * size
                acc[pl.ds(at, half, stride=2), :] = total[:half]
                acc[pl.ds(at + 1, half, stride=2), :] = total[half:]

    each(n, find_route)
    pl.semaphore_wait(
        barrier,
        n - 1 + jnp.where(ry > 0, 1, 0) + jnp.where(ry < ny - 1, 1, 0),
    )

    def start_halo(signal, hop):
        for sends, gets, copy in halo_copies(signal, hop):
            pl.when(sends)(copy.start)

    def wait_halo(signal, hop):
        for sends, gets, copy in halo_copies(signal, hop):
            pl.when(gets)(copy.wait_recv)

    each(n - 1, lambda k: send_targets(k, False))
    send_targets(n - 1, True)
    fetches[0].wait()
    for i in range(br):
        gated[i] = gate(cell[i].reshape(bc * size, feats)).reshape(bc, size, feats)
    start_halo(gated, 0)
    send_far(gated, 0)

    low = lax.broadcasted_iota(jnp.int32, (half, 2 * size), 1) < size

    def arrange(i):
        slot = lax.rem(i, spread.shape[0])
        for k in range(5):
            for r in range(half):
                piece = adjacency[i, k, :, r * 2 * size : (r + 1) * 2 * size]
                at = r * 8 + k % 2 * bc
                spread[slot, k // 2, at : at + bc] = piece.astype(F32)
        for j in range(bc):
            pairs = [
                spread[slot, k // 2, pl.ds(k % 2 * bc + j, half, stride=8), :] for k in range(5)
            ]
            turned = [pltpu.roll(pair, size, 1) for pair in pairs]
            zero = jnp.zeros_like(pairs[0])
            pairs.append(zero)
            turned.append(zero)
            for k in range(0, 6, 2):
                span = slice(k * size, (k + 2) * size)
                even = jnp.where(low, pairs[k], turned[k + 1])
                odd = jnp.where(low, turned[k], pairs[k + 1])
                tiles[i * bc + j, :half, span] = even.astype(BF16)
                tiles[i * bc + j, half:, span] = odd.astype(BF16)

    fetches[5].wait()
    blocks_loop(br, arrange, 2)

    wait_halo(gated, 0)
    near(gated, 0)

    def wait_target(k):
        source = lax.rem(rx + n - k - 1, n)
        target_copy(source, source).wait_recv()

    each(n - 1, wait_target)
    spot = lax.broadcasted_iota(jnp.int32, (size, CAP * size), 1) % size
    row = lax.broadcasted_iota(jnp.int32, (size, CAP * size), 0)
    unit = jnp.where(row == 2 * (spot % half) + spot // half, 1.0, 0.0).astype(BF16)
    for source in range(n):
        named = target_recv[source, 0:1]
        span = slice(source % 2 * CAP * size, (source % 2 + 1) * CAP * size)
        for block in range(blocks):
            hit = jnp.where(named == float(block), 1.0, 0.0).astype(BF16)
            select[source // 2, block * size : (block + 1) * size, span] = unit * hit

    strip = bc * size

    def end_first(i, total):
        first[i] = total.astype(BF16).reshape(bc, size, feats)

    add_far(0, end_first)
    start_halo(first, 1)
    send_far(first, 1)

    for i in range(br):
        known = [gated[i].reshape(strip, feats), first[i].reshape(strip, feats)]
        own = dot(jnp.concatenate(known, axis=1), early_mix) + bias_table[2:3]
        base[i * strip : (i + 1) * strip] = own + cell[i].reshape(strip, feats).astype(F32)
    wait_halo(first, 1)
    near(first, 1)

    def end_second(i, second):
        upper = second.astype(BF16)
        lower = (second - upper.astype(F32)).astype(BF16)
        total = base[i * strip : (i + 1) * strip]
        total = total + dot(jnp.concatenate([upper, lower], axis=1), late_mix)
        out[i] = total.astype(BF16).reshape(bc, size, feats)

    add_far(1, end_second)

    for hop, signal in enumerate((gated, first)):
        for sends, gets, copy in halo_copies(signal, hop):
            pl.when(sends)(copy.wait_send)

        def sent(k):
            d = destination(k)
            far_copy(hop, d, rx).wait_send()
            if hop == 0:
                target_copy(d, rx).wait_send()

        each(n - 1, sent)


def local(
    n,
    ny,
    cell_input,
    w_filter,
    w_gate,
    bias_filter,
    bias_gate,
    adjacency,
    out_block,
    out_dev,
    out_target,
    out_tiles,
    w_mix,
    bias_mix,
):
    br, bc, size, feats = cell_input.shape
    blocks = br * bc
    rows = blocks * size
    edges = out_tiles.shape[2]
    channels = w_filter.shape[1]
    half = size // 2
    stride = -(-edges // 8) * 8
    assert feats == 128 and size == 64 and br == bc == 4 and n % 4 == 0
    vmem = pl.BlockSpec(memory_space=pltpu.VMEM)
    dma = pltpu.SemaphoreType.DMA
    hbm = pl.BlockSpec(memory_space=pltpu.HBM)
    operands = (
        cell_input,
        w_filter,
        w_gate,
        bias_filter.reshape(1, channels),
        bias_gate.reshape(1, channels),
        adjacency.transpose(0, 2, 1, 3),
        out_block,
        out_dev.reshape(out_block.shape),
        out_target,
        out_tiles,
        w_mix,
        bias_mix.reshape(1, channels),
    )
    scratch = [
        (pltpu.SMEM if k in (6, 7, 8) else pltpu.VMEM)(a.shape, a.dtype)
        for k, a in enumerate(operands)
    ] + [
        pltpu.VMEM((br, bc, size, feats), BF16),
        pltpu.VMEM((br, bc, size, feats), BF16),
        pltpu.VMEM((2, 2, bc, size, feats), BF16),
        pltpu.VMEM((2, 2, br, size, feats), BF16),
        pltpu.VMEM((2, n, CAP * size, feats), BF16),
        pltpu.VMEM((2, n, CAP * size, feats), BF16),
        pltpu.VMEM((n, 8, CAP * size), F32),
        pltpu.VMEM((n, 8, CAP * size), F32),
        pltpu.VMEM((n // 2, rows, 2 * CAP * size), BF16),
        pltpu.VMEM((blocks, size, 6 * size), BF16),
        pltpu.VMEM((edges, size, 2 * size), BF16),
        pltpu.VMEM((2, 3, half * 8, 2 * size), F32),
        pltpu.VMEM((half * stride, 2 * size), F32),
        pltpu.VMEM((feats, 5 * feats), F32),
        pltpu.VMEM((8, feats), F32),
        pltpu.VMEM((rows, feats), F32),
        pltpu.VMEM((rows, feats), F32),
        dma((2, n)),
        dma((2, n)),
        dma((n,)),
        dma((n,)),
        dma((2, 2, 2)),
        dma((2, 2, 2)),
        dma((12,)),
        pltpu.SMEM((n, 3 * CAP), jnp.int32),
    ]
    near_flops = 2 * 2 * 5 * rows * size * feats
    return pl.pallas_call(
        functools.partial(kernel, n, ny),
        out_shape=jax.ShapeDtypeStruct(cell_input.shape, BF16),
        in_specs=[hbm] * 12,
        out_specs=vmem,
        scratch_shapes=scratch,
        cost_estimate=pl.CostEstimate(
            flops=near_flops, bytes_accessed=2 * rows * feats * 2, transcendentals=2 * rows * feats
        ),
        compiler_params=pltpu.CompilerParams(
            collective_id=0, has_side_effects=True, vmem_limit_bytes=40 * 1024 * 1024
        ),
    )(*(pltpu.with_memory_space_constraint(a, pltpu.HBM) for a in operands))


def solution(mesh):
    in_specs = (
        P("rx", "ry", None, None),
        P(),
        P(),
        P(),
        P(),
        P("rx", "ry", None, None),
        P("rx", "ry", None),
        P("rx", "ry", None, None),
        P("rx", "ry", None),
        P("rx", "ry", None, None),
        P(),
        P(),
    )
    out_specs = P("rx", "ry", None, None)
    body = functools.partial(local, mesh.shape["rx"], mesh.shape["ry"])
    return jax.shard_map(body, mesh=mesh, in_specs=in_specs, out_specs=out_specs, check_vma=False)
```

```python
import functools

import jax
import jax.numpy as jnp
from jax import lax
from jax.experimental import pallas as pl
from jax.experimental.pallas import tpu as pltpu
from jax.sharding import PartitionSpec as P

DILATION_STEP = 2
CAP = 2
MESH = pl.DeviceIdType.MESH
F32 = jnp.float32
BF16 = jnp.bfloat16


def dot(a, b):
    return jnp.dot(a, b, preferred_element_type=F32)


def each(count, body, limit=8):
    if count <= limit:
        for k in range(count):
            body(k)
    else:

        def step(k, carry):
            body(k)
            return carry

        lax.fori_loop(0, count, step, 0)


def blocks_loop(count, body, unroll):
    def step(k, carry):
        body(k)
        return carry

    lax.fori_loop(0, count, step, 0, unroll=unroll)


def kernel(
    n,
    ny,
    *refs,
):
    inputs, (out, *landing), refs = refs[:12], refs[12:25], refs[25:]
    (
        cell,
        w_filter,
        w_gate,
        bias_filter,
        bias_gate,
        adjacency,
        out_block,
        out_dev,
        out_target,
        out_tiles,
        w_mix,
        bias_mix,
    ) = landing
    (
    gated,
    first,
    halo_rows,
    halo_cols,
    send_buf,
    recv_buf,
    target_send,
    target_recv,
    select,
    tiles,
    edge_tiles,
    spread,
    edge_spread,
    table,
    bias_table,
    acc,
    base,
    send_sem,
    recv_sem,
    target_send_sem,
    target_recv_sem,
    halo_send_sem,
    halo_recv_sem,
    fetch_sem,
    route,
    ) = refs
    fetches = [
        pltpu.make_async_copy(src, dst, fetch_sem.at[k])
        for k, (src, dst) in enumerate(zip(inputs, landing))
    ]
    for k in (1, 2, 3, 4, 0, 9, 6, 7, 8, 10, 11, 5):
        fetches[k].start()
    br, bc, size, feats = cell.shape
    blocks = br * bc
    rows = blocks * size
    half = size // 2
    edges = out_tiles.shape[2]
    channels = w_filter.shape[1]
    steps = feats // channels
    stride = edge_spread.shape[0] // half
    rx = lax.axis_index("rx")
    ry = lax.axis_index("ry")

    barrier = pltpu.get_barrier_semaphore()

    def greet(k):
        pl.semaphore_signal(
            barrier, inc=1, device_id={"rx": lax.rem(rx + k + 1, n)}, device_id_type=MESH
        )

    each(n - 1, greet)

    @pl.when(ry > 0)
    def _():
        pl.semaphore_signal(barrier, inc=1, device_id={"ry": ry - 1}, device_id_type=MESH)

    @pl.when(ry < ny - 1)
    def _():
        pl.semaphore_signal(barrier, inc=1, device_id={"ry": ry + 1}, device_id_type=MESH)

    def halo_copies(signal, hop):
        sides = []
        for which, (axis, here, count, halo) in enumerate(
            (("rx", rx, n, halo_rows), ("ry", ry, ny, halo_cols))
        ):
            last = (br if which == 0 else bc) - 1
            for side, (edge, step) in enumerate(((last, 1), (0, -1))):
                src = signal.at[edge] if which == 0 else signal.at[:, edge]
                copy = pltpu.make_async_remote_copy(
                    src_ref=src,
                    dst_ref=halo.at[2 - hop, side],
                    send_sem=halo_send_sem.at[hop, which, side],
                    recv_sem=halo_recv_sem.at[hop, which, side],
                    device_id={axis: jnp.clip(here + step, 0, count - 1)},
                    device_id_type=MESH,
                )
                sends = (here < count - 1) if step == 1 else (here > 0)
                gets = (here > 0) if step == 1 else (here < count - 1)
                sides.append((sends, gets, copy))
        return sides

    def start_halo(signal, hop, axes=(0, 1)):
        for which in axes:
            for sends, gets, copy in halo_copies(signal, hop)[2 * which : 2 * which + 2]:
                pl.when(sends)(copy.start)

    def wait_halo(signal, hop):
        for sends, gets, copy in halo_copies(signal, hop):
            pl.when(gets)(copy.wait_recv)

    pl.semaphore_wait(
        barrier,
        n - 1 + jnp.where(ry > 0, 1, 0) + jnp.where(ry < ny - 1, 1, 0),
    )

    zero_side = jnp.zeros((2,) + halo_rows.shape[2:], BF16)

    @pl.when(rx == 0)
    def _():
        halo_rows[1:, 0] = zero_side

    @pl.when(rx == n - 1)
    def _():
        halo_rows[1:, 1] = zero_side

    @pl.when(ry == 0)
    def _():
        halo_cols[1:, 0] = zero_side

    @pl.when(ry == ny - 1)
    def _():
        halo_cols[1:, 1] = zero_side

    start_halo(inputs[0], 0)
    for k in range(1, 5):
        fetches[k].wait()
    for k in (10, 11):
        fetches[k].wait()

    table[...] = jnp.zeros_like(table)
    for t in range(steps):
        span = slice(t * channels, (t + 1) * channels)
        for which, weights in enumerate((w_filter, w_gate)):
            for tap, to in ((1, t), (0, t + DILATION_STEP)):
                if to < steps:
                    at = which * feats + to * channels
                    table[span, at : at + channels] = weights[tap].astype(F32)
        for hop in range(3):
            at = (2 + hop) * feats + t * channels
            table[span, at : at + channels] = w_mix[hop].astype(F32)
        bias_table[0:1, span] = bias_filter[...]
        bias_table[1:2, span] = bias_gate[...]
        bias_table[2:3, span] = bias_mix[...]
    taps = table[:, : 2 * feats].astype(BF16)
    mixes = [table[:, (2 + h) * feats : (3 + h) * feats].astype(BF16) for h in range(3)]
    early_mix = jnp.concatenate(mixes[:2], axis=0)
    late_mix = jnp.concatenate([mixes[2], mixes[2]], axis=0)

    def gate(block_rows):
        pre = dot(block_rows, taps)
        pre_f = pre[:, :feats] + bias_table[0:1]
        pre_g = pre[:, feats:] + bias_table[1:2]
        value = jnp.tanh(pre_f) * (0.5 * jnp.tanh(0.5 * pre_g) + 0.5)
        return value.astype(BF16)

    fetches[0].wait()
    for i in range(br):
        gated[i] = gate(cell[i].reshape(bc * size, feats)).reshape(bc, size, feats)

    for k in range(6, 10):
        fetches[k].wait()

    for r in range(half):
        piece = out_tiles[0, 0, :, r * 2 * size : (r + 1) * 2 * size]
        edge_spread[r * stride : r * stride + edges] = piece.astype(F32)
    for e in range(edges):
        pairs = edge_spread[pl.ds(e, half, stride=stride), :]
        edge_tiles[e, :half] = pairs.astype(BF16)
        edge_tiles[e, half:] = pltpu.roll(pairs, size, 1).astype(BF16)

    part = n // 2

    def destination(k):
        side = (rx // part + 1 + k // part) % 2
        return side * part + (rx % part + k % part + 1) % part

    lane = lax.broadcasted_iota(jnp.int32, (1, CAP * size), 1)

    def far_copy(hop, d, source):
        return pltpu.make_async_remote_copy(
            src_ref=send_buf.at[hop, d],
            dst_ref=recv_buf.at[hop, source],
            send_sem=send_sem.at[hop, d],
            recv_sem=recv_sem.at[hop, source],
            device_id={"rx": d},
            device_id_type=MESH,
        )

    def target_copy(d, source):
        return pltpu.make_async_remote_copy(
            src_ref=target_send.at[d],
            dst_ref=target_recv.at[source],
            send_sem=target_send_sem.at[d],
            recv_sem=target_recv_sem.at[source],
            device_id={"rx": d},
            device_id_type=MESH,
        )

    def find_route(k):
        d = destination(k)
        head, tail = jnp.int32(-1), jnp.int32(-1)
        for e in range(edges):
            hit = out_dev[0, 0, e] == d
            head = jnp.where(hit & (head < 0), e, head)
            tail = jnp.where(hit, e, tail)
        found = ((head, head >= 0), (tail, tail != head))
        for c, (index, valid) in enumerate(found):
            index = jnp.maximum(index, 0)
            route[k, c] = index
            route[k, CAP + c] = out_block[0, 0, index]
            route[k, 2 * CAP + c] = jnp.where(valid, 1, 0)

    def send_targets(k, own):
        d = destination(k)
        names = [
            jnp.where(route[k, 2 * CAP + c] == 1, out_target[0, 0, route[k, c]], -1)
            for c in range(CAP)
        ]
        named = jnp.where(lane < size, names[0], names[1]).astype(F32)
        if own:
            target_recv[rx] = named
        else:
            target_send[d] = named
            target_copy(d, rx).start()

    team = 4

    def send_group(signal, hop, start, last):
        ks = [start + g for g in range(team)]
        picked = []
        for k in ks:
            for c in range(CAP):
                b = route[k, CAP + c]
                picked.append(signal[lax.div(b, bc), lax.rem(b, bc)])
        sums = []
        for g, k in enumerate(ks):
            for c in range(CAP):
                product = dot(edge_tiles[route[k, c]][:, :size], picked[g * CAP + c])
                sums.append((product * route[k, 2 * CAP + c].astype(F32)).astype(BF16))
        for g, k in enumerate(ks):
            both = jnp.concatenate(sums[g * CAP : (g + 1) * CAP], axis=0)
            if last and g == team - 1:
                recv_buf[hop, rx] = both
            else:
                send_buf[hop, destination(k)] = both
        for g, k in enumerate(ks):
            if not (last and g == team - 1):
                far_copy(hop, destination(k), rx).start()

    def send_far(signal, hop):
        each(n // team - 1, lambda g: send_group(signal, hop, g * team, False))
        send_group(signal, hop, n - team, True)

    part_pairs = n // 4

    def add_far(hop, finish):
        strip = bc * size

        def wait_source(source):
            far_copy(hop, source, source).wait_recv()

        def one(q):
            side = (rx // part + q // part_pairs) % 2
            pair = side * part_pairs + (rx % part // 2 + q % part_pairs) % part_pairs
            if isinstance(q, int) and q == 0:
                wait_source(rx + 1 - 2 * (rx % 2))
            else:
                wait_source(2 * pair)
                wait_source(2 * pair + 1)
            landed = recv_buf[hop, pl.ds(2 * pair, 2)].reshape(2 * CAP * size, feats)
            for i in (0, br - 1, *range(1, br - 1)):
                span = slice(i * strip, (i + 1) * strip)
                total = acc[span] + dot(select[pair, span], landed)
                if isinstance(q, int) and q == n // 2 - 1:
                    finish(i, total)
                else:
                    acc[span] = total

        one(0)
        each(n // 2 - 2, lambda q: one(q + 1))
        one(n // 2 - 1)

    def near(signal, hop):
        for i in range(br):
            for j in range(bc):
                up = signal[i - 1, j] if i > 0 else halo_rows[hop, 0, j]
                down = signal[i + 1, j] if i < br - 1 else halo_rows[hop, 1, j]
                left = signal[i, j - 1] if j > 0 else halo_cols[hop, 0, i]
                right = signal[i, j + 1] if j < bc - 1 else halo_cols[hop, 1, i]
                column = jnp.concatenate([signal[i, j], up, down, left, right], axis=0)
                total = dot(tiles[i * bc + j][:, : 5 * size], column)
                at = (i * bc + j) * size
                acc[pl.ds(at, half, stride=2), :] = total[:half]
                acc[pl.ds(at + 1, half, stride=2), :] = total[half:]

    each(n, find_route)
    each(n - 1, lambda k: send_targets(k, False))
    send_targets(n - 1, True)
    send_far(gated, 0)

    low = lax.broadcasted_iota(jnp.int32, (half, 2 * size), 1) < size

    def arrange(i):
        slot = lax.rem(i, spread.shape[0])
        for k in range(5):
            for r in range(half):
                piece = adjacency[i, k, :, r * 2 * size : (r + 1) * 2 * size]
                at = r * 8 + k % 2 * bc
                spread[slot, k // 2, at : at + bc] = piece.astype(F32)
        for j in range(bc):
            pairs = [
                spread[slot, k // 2, pl.ds(k % 2 * bc + j, half, stride=8), :] for k in range(5)
            ]
            turned = [pltpu.roll(pair, size, 1) for pair in pairs]
            zero = jnp.zeros_like(pairs[0])
            pairs.append(zero)
            turned.append(zero)
            for k in range(0, 6, 2):
                span = slice(k * size, (k + 2) * size)
                even = jnp.where(low, pairs[k], turned[k + 1])
                odd = jnp.where(low, turned[k], pairs[k + 1])
                tiles[i * bc + j, :half, span] = even.astype(BF16)
                tiles[i * bc + j, half:, span] = odd.astype(BF16)

    fetches[5].wait()
    blocks_loop(br, arrange, 2)

    wait_halo(inputs[0], 0)
    inside = ((rx > 0, rx < n - 1), (ry > 0, ry < ny - 1))
    for which, halo in enumerate((halo_rows, halo_cols)):
        for side in range(2):
            values = gate(halo[2, side].reshape(bc * size, feats))
            kept = values * jnp.where(inside[which][side], 1.0, 0.0).astype(BF16)
            halo[0, side] = kept.reshape(bc, size, feats)
    near(gated, 0)

    def wait_target(k):
        source = lax.rem(rx + n - k - 1, n)
        target_copy(source, source).wait_recv()

    each(n - 1, wait_target)
    spot = lax.broadcasted_iota(jnp.int32, (size, CAP * size), 1) % size
    row = lax.broadcasted_iota(jnp.int32, (size, CAP * size), 0)
    unit = jnp.where(row == 2 * (spot % half) + spot // half, 1.0, 0.0).astype(BF16)
    for source in range(n):
        named = target_recv[source, 0:1]
        span = slice(source % 2 * CAP * size, (source % 2 + 1) * CAP * size)
        for block in range(blocks):
            hit = jnp.where(named == float(block), 1.0, 0.0).astype(BF16)
            select[source // 2, block * size : (block + 1) * size, span] = unit * hit

    strip = bc * size

    def end_first(i, total):
        first[i] = total.astype(BF16).reshape(bc, size, feats)
        if i == br - 1:
            start_halo(first, 1, (0,))

    add_far(0, end_first)
    start_halo(first, 1, (1,))
    send_far(first, 1)

    for i in range(br):
        known = [gated[i].reshape(strip, feats), first[i].reshape(strip, feats)]
        own = dot(jnp.concatenate(known, axis=1), early_mix) + bias_table[2:3]
        base[i * strip : (i + 1) * strip] = own + cell[i].reshape(strip, feats).astype(F32)
    wait_halo(first, 1)
    near(first, 1)

    def end_second(i, second):
        upper = second.astype(BF16)
        lower = (second - upper.astype(F32)).astype(BF16)
        total = base[i * strip : (i + 1) * strip]
        total = total + dot(jnp.concatenate([upper, lower], axis=1), late_mix)
        out[i] = total.astype(BF16).reshape(bc, size, feats)

    add_far(1, end_second)

    for hop, signal in enumerate((inputs[0], first)):
        for sends, gets, copy in halo_copies(signal, hop):
            pl.when(sends)(copy.wait_send)

        def sent(k):
            d = destination(k)
            far_copy(hop, d, rx).wait_send()
            if hop == 0:
                target_copy(d, rx).wait_send()

        each(n - 1, sent)


def local(
    n,
    ny,
    cell_input,
    w_filter,
    w_gate,
    bias_filter,
    bias_gate,
    adjacency,
    out_block,
    out_dev,
    out_target,
    out_tiles,
    w_mix,
    bias_mix,
):
    br, bc, size, feats = cell_input.shape
    blocks = br * bc
    rows = blocks * size
    edges = out_tiles.shape[2]
    channels = w_filter.shape[1]
    half = size // 2
    stride = -(-edges // 8) * 8
    assert feats == 128 and size == 64 and br == bc == 4 and n % 4 == 0
    vmem = pl.BlockSpec(memory_space=pltpu.VMEM)
    dma = pltpu.SemaphoreType.DMA
    hbm = pl.BlockSpec(memory_space=pltpu.HBM)
    operands = (
        cell_input,
        w_filter,
        w_gate,
        bias_filter.reshape(1, channels),
        bias_gate.reshape(1, channels),
        adjacency.transpose(0, 2, 1, 3),
        out_block,
        out_dev.reshape(out_block.shape),
        out_target,
        out_tiles,
        w_mix,
        bias_mix.reshape(1, channels),
    )
    scratch = [
        (pltpu.SMEM if k in (6, 7, 8) else pltpu.VMEM)(a.shape, a.dtype)
        for k, a in enumerate(operands)
    ] + [
        pltpu.VMEM((br, bc, size, feats), BF16),
        pltpu.VMEM((br, bc, size, feats), BF16),
        pltpu.VMEM((3, 2, bc, size, feats), BF16),
        pltpu.VMEM((3, 2, br, size, feats), BF16),
        pltpu.VMEM((2, n, CAP * size, feats), BF16),
        pltpu.VMEM((2, n, CAP * size, feats), BF16),
        pltpu.VMEM((n, 1, CAP * size), F32),
        pltpu.VMEM((n, 1, CAP * size), F32),
        pltpu.VMEM((n // 2, rows, 2 * CAP * size), BF16),
        pltpu.VMEM((blocks, size, 6 * size), BF16),
        pltpu.VMEM((edges, size, 2 * size), BF16),
        pltpu.VMEM((2, 3, half * 8, 2 * size), F32),
        pltpu.VMEM((half * stride, 2 * size), F32),
        pltpu.VMEM((feats, 5 * feats), F32),
        pltpu.VMEM((8, feats), F32),
        pltpu.VMEM((rows, feats), F32),
        pltpu.VMEM((rows, feats), F32),
        dma((2, n)),
        dma((2, n)),
        dma((n,)),
        dma((n,)),
        dma((2, 2, 2)),
        dma((2, 2, 2)),
        dma((12,)),
        pltpu.SMEM((n, 3 * CAP), jnp.int32),
    ]
    near_flops = 2 * 2 * 5 * rows * size * feats
    return pl.pallas_call(
        functools.partial(kernel, n, ny),
        out_shape=jax.ShapeDtypeStruct(cell_input.shape, BF16),
        in_specs=[hbm] * 12,
        out_specs=vmem,
        scratch_shapes=scratch,
        cost_estimate=pl.CostEstimate(
            flops=near_flops, bytes_accessed=2 * rows * feats * 2, transcendentals=2 * rows * feats
        ),
        compiler_params=pltpu.CompilerParams(
            collective_id=0, has_side_effects=True, vmem_limit_bytes=40 * 1024 * 1024
        ),
    )(*(pltpu.with_memory_space_constraint(a, pltpu.HBM) for a in operands))


def solution(mesh):
    in_specs = (
        P("rx", "ry", None, None),
        P(),
        P(),
        P(),
        P(),
        P("rx", "ry", None, None),
        P("rx", "ry", None),
        P("rx", "ry", None, None),
        P("rx", "ry", None),
        P("rx", "ry", None, None),
        P(),
        P(),
    )
    out_specs = P("rx", "ry", None, None)
    body = functools.partial(local, mesh.shape["rx"], mesh.shape["ry"])
    return jax.shard_map(body, mesh=mesh, in_specs=in_specs, out_specs=out_specs, check_vma=False)
```

```python
import functools

import jax
import jax.numpy as jnp
from jax import lax
from jax.experimental import pallas as pl
from jax.experimental.pallas import tpu as pltpu
from jax.sharding import PartitionSpec as P

DILATION_STEP = 2
CAP = 2
MESH = pl.DeviceIdType.MESH
F32 = jnp.float32
BF16 = jnp.bfloat16


def dot(a, b):
    return jnp.dot(a, b, preferred_element_type=F32)


def each(count, body, limit=8):
    if count <= limit:
        for k in range(count):
            body(k)
    else:

        def step(k, carry):
            body(k)
            return carry

        lax.fori_loop(0, count, step, 0)


def blocks_loop(count, body, unroll):
    def step(k, carry):
        body(k)
        return carry

    lax.fori_loop(0, count, step, 0, unroll=unroll)


def kernel(
    n,
    ny,
    *refs,
):
    inputs, (out, *landing), refs = refs[:12], refs[12:25], refs[25:]
    (
        cell,
        w_filter,
        w_gate,
        bias_filter,
        bias_gate,
        adjacency,
        out_block,
        out_dev,
        out_target,
        out_tiles,
        w_mix,
        bias_mix,
    ) = landing
    (
    gated,
    first,
    halo_rows,
    halo_cols,
    send_buf,
    recv_buf,
    target_send,
    target_recv,
    select,
    tiles,
    edge_tiles,
    spread,
    edge_spread,
    table,
    bias_table,
    acc,
    base,
    send_sem,
    recv_sem,
    target_send_sem,
    target_recv_sem,
    halo_send_sem,
    halo_recv_sem,
    fetch_sem,
    route,
    ) = refs
    fetches = [
        pltpu.make_async_copy(src, dst, fetch_sem.at[k])
        for k, (src, dst) in enumerate(zip(inputs, landing))
    ]
    for k in (6, 7, 8, 1, 2, 3, 4, 9, 0, 10, 11, 5):
        fetches[k].start()
    br, bc, size, feats = cell.shape
    blocks = br * bc
    rows = blocks * size
    half = size // 2
    edges = out_tiles.shape[2]
    channels = w_filter.shape[1]
    steps = feats // channels
    stride = edge_spread.shape[0] // half
    rx = lax.axis_index("rx")
    ry = lax.axis_index("ry")

    barrier = pltpu.get_barrier_semaphore()

    def greet(k):
        pl.semaphore_signal(
            barrier, inc=1, device_id={"rx": lax.rem(rx + k + 1, n)}, device_id_type=MESH
        )

    each(n - 1, greet)

    @pl.when(ry > 0)
    def _():
        pl.semaphore_signal(barrier, inc=1, device_id={"ry": ry - 1}, device_id_type=MESH)

    @pl.when(ry < ny - 1)
    def _():
        pl.semaphore_signal(barrier, inc=1, device_id={"ry": ry + 1}, device_id_type=MESH)

    def halo_copies(signal, hop):
        sides = []
        for which, (axis, here, count, halo) in enumerate(
            (("rx", rx, n, halo_rows), ("ry", ry, ny, halo_cols))
        ):
            last = (br if which == 0 else bc) - 1
            for side, (edge, step) in enumerate(((last, 1), (0, -1))):
                src = signal.at[edge] if which == 0 else signal.at[:, edge]
                copy = pltpu.make_async_remote_copy(
                    src_ref=src,
                    dst_ref=halo.at[2 - hop if which == 0 else hop, side],
                    send_sem=halo_send_sem.at[hop, which, side],
                    recv_sem=halo_recv_sem.at[hop, which, side],
                    device_id={axis: jnp.clip(here + step, 0, count - 1)},
                    device_id_type=MESH,
                )
                sends = (here < count - 1) if step == 1 else (here > 0)
                gets = (here > 0) if step == 1 else (here < count - 1)
                sides.append((sends, gets, copy))
        return sides

    def start_halo(signal, hop, axes=(0, 1)):
        for which in axes:
            for sends, gets, copy in halo_copies(signal, hop)[2 * which : 2 * which + 2]:
                pl.when(sends)(copy.start)

    def wait_halo(signal, hop, axes=(0, 1)):
        for which in axes:
            for sends, gets, copy in halo_copies(signal, hop)[2 * which : 2 * which + 2]:
                pl.when(gets)(copy.wait_recv)

    pl.semaphore_wait(
        barrier,
        n - 1 + jnp.where(ry > 0, 1, 0) + jnp.where(ry < ny - 1, 1, 0),
    )

    zero_side = jnp.zeros((2,) + halo_rows.shape[2:], BF16)

    @pl.when(rx == 0)
    def _():
        halo_rows[1:, 0] = zero_side

    @pl.when(rx == n - 1)
    def _():
        halo_rows[1:, 1] = zero_side

    @pl.when(ry == 0)
    def _():
        halo_cols[:, 0] = zero_side

    @pl.when(ry == ny - 1)
    def _():
        halo_cols[:, 1] = zero_side

    start_halo(inputs[0], 0, (0,))
    for k in range(1, 5):
        fetches[k].wait()

    table[...] = jnp.zeros_like(table)
    for t in range(steps):
        span = slice(t * channels, (t + 1) * channels)
        for which, weights in enumerate((w_filter, w_gate)):
            for tap, to in ((1, t), (0, t + DILATION_STEP)):
                if to < steps:
                    at = which * feats + to * channels
                    table[span, at : at + channels] = weights[tap].astype(F32)
        bias_table[0:1, span] = bias_filter[...]
        bias_table[1:2, span] = bias_gate[...]
    taps = table[:, : 2 * feats].astype(BF16)

    def gate(block_rows):
        pre = dot(block_rows, taps)
        pre_f = pre[:, :feats] + bias_table[0:1]
        pre_g = pre[:, feats:] + bias_table[1:2]
        value = jnp.tanh(pre_f) * (0.5 * jnp.tanh(0.5 * pre_g) + 0.5)
        return value.astype(BF16)

    for k in range(6, 10):
        fetches[k].wait()

    for r in range(half):
        piece = out_tiles[0, 0, :, r * 2 * size : (r + 1) * 2 * size]
        edge_spread[r * stride : r * stride + edges] = piece.astype(F32)
    for e in range(edges):
        pairs = edge_spread[pl.ds(e, half, stride=stride), :]
        edge_tiles[e, :half] = pairs.astype(BF16)
        edge_tiles[e, half:] = pltpu.roll(pairs, size, 1).astype(BF16)

    part = n // 2

    def destination(k):
        side = (rx // part + 1 + k // part) % 2
        return side * part + (rx % part + k % part + 1) % part

    lane = lax.broadcasted_iota(jnp.int32, (1, CAP * size), 1)

    def far_copy(hop, d, source):
        return pltpu.make_async_remote_copy(
            src_ref=send_buf.at[hop, d],
            dst_ref=recv_buf.at[hop, source],
            send_sem=send_sem.at[hop, d],
            recv_sem=recv_sem.at[hop, source],
            device_id={"rx": d},
            device_id_type=MESH,
        )

    def target_copy(d, source):
        return pltpu.make_async_remote_copy(
            src_ref=target_send.at[d],
            dst_ref=target_recv.at[source],
            send_sem=target_send_sem.at[d],
            recv_sem=target_recv_sem.at[source],
            device_id={"rx": d},
            device_id_type=MESH,
        )

    def find_route(k):
        d = destination(k)
        head, tail = jnp.int32(-1), jnp.int32(-1)
        for e in range(edges):
            hit = out_dev[0, 0, e] == d
            head = jnp.where(hit & (head < 0), e, head)
            tail = jnp.where(hit, e, tail)
        found = ((head, head >= 0), (tail, tail != head))
        for c, (index, valid) in enumerate(found):
            index = jnp.maximum(index, 0)
            route[k, c] = index
            route[k, CAP + c] = out_block[0, 0, index]
            route[k, 2 * CAP + c] = jnp.where(valid, 1, 0)

    def send_targets(k, own):
        d = destination(k)
        names = [
            jnp.where(route[k, 2 * CAP + c] == 1, out_target[0, 0, route[k, c]], -1)
            for c in range(CAP)
        ]
        named = jnp.where(lane < size, names[0], names[1]).astype(F32)
        if own:
            target_recv[rx] = named
        else:
            target_send[d] = named
            target_copy(d, rx).start()

    team = 4

    def send_group(signal, hop, start, last, gating):
        ks = [start + g for g in range(team)]
        picked = []
        for k in ks:
            for c in range(CAP):
                b = route[k, CAP + c]
                picked.append(signal[lax.div(b, bc), lax.rem(b, bc)])
        if gating:
            gates = gate(jnp.concatenate(picked, axis=0))
            picked = [gates[p * size : (p + 1) * size] for p in range(team * CAP)]
        sums = []
        for g, k in enumerate(ks):
            for c in range(CAP):
                product = dot(edge_tiles[route[k, c]][:, :size], picked[g * CAP + c])
                sums.append((product * route[k, 2 * CAP + c].astype(F32)).astype(BF16))
        for g, k in enumerate(ks):
            both = jnp.concatenate(sums[g * CAP : (g + 1) * CAP], axis=0)
            if last and g == team - 1:
                recv_buf[hop, rx] = both
            else:
                send_buf[hop, destination(k)] = both
        for g, k in enumerate(ks):
            if not (last and g == team - 1):
                far_copy(hop, destination(k), rx).start()

    def send_rest(signal, hop):
        each(n // team - 2, lambda g: send_group(signal, hop, (g + 1) * team, False, False))
        send_group(signal, hop, n - team, True, False)

    part_pairs = n // 4

    def add_far(hop, finish):
        strip = bc * size

        def wait_source(source):
            far_copy(hop, source, source).wait_recv()

        def one(q):
            side = (rx // part + q // part_pairs) % 2
            pair = side * part_pairs + (rx % part // 2 + q % part_pairs) % part_pairs
            if isinstance(q, int) and q == 0:
                wait_source(rx + 1 - 2 * (rx % 2))
            else:
                wait_source(2 * pair)
                wait_source(2 * pair + 1)
            landed = recv_buf[hop, pl.ds(2 * pair, 2)].reshape(2 * CAP * size, feats)
            for i in (0, br - 1, *range(1, br - 1)):
                span = slice(i * strip, (i + 1) * strip)
                total = acc[span] + dot(select[pair, span], landed)
                if isinstance(q, int) and q == n // 2 - 1:
                    finish(i, total)
                else:
                    acc[span] = total

        one(0)
        each(n // 2 - 2, lambda q: one(q + 1))
        one(n // 2 - 1)

    def near(signal, hop):
        for i in range(br):
            for j in range(bc):
                up = signal[i - 1, j] if i > 0 else halo_rows[hop, 0, j]
                down = signal[i + 1, j] if i < br - 1 else halo_rows[hop, 1, j]
                left = signal[i, j - 1] if j > 0 else halo_cols[hop, 0, i]
                right = signal[i, j + 1] if j < bc - 1 else halo_cols[hop, 1, i]
                column = jnp.concatenate([signal[i, j], up, down, left, right], axis=0)
                total = dot(tiles[i * bc + j][:, : 5 * size], column)
                at = (i * bc + j) * size
                acc[pl.ds(at, half, stride=2), :] = total[:half]
                acc[pl.ds(at + 1, half, stride=2), :] = total[half:]

    each(n, find_route)
    fetches[0].wait()
    send_group(cell, 0, 0, False, True)
    for i in range(br):
        gated[i] = gate(cell[i].reshape(bc * size, feats)).reshape(bc, size, feats)
    start_halo(gated, 0, (1,))
    send_rest(gated, 0)
    each(n - 1, lambda k: send_targets(k, False))
    send_targets(n - 1, True)

    low = lax.broadcasted_iota(jnp.int32, (half, 2 * size), 1) < size

    def arrange(i):
        slot = lax.rem(i, spread.shape[0])
        for k in range(5):
            for r in range(half):
                piece = adjacency[i, k, :, r * 2 * size : (r + 1) * 2 * size]
                at = r * 8 + k % 2 * bc
                spread[slot, k // 2, at : at + bc] = piece.astype(F32)
        for j in range(bc):
            pairs = [
                spread[slot, k // 2, pl.ds(k % 2 * bc + j, half, stride=8), :] for k in range(5)
            ]
            turned = [pltpu.roll(pair, size, 1) for pair in pairs]
            zero = jnp.zeros_like(pairs[0])
            pairs.append(zero)
            turned.append(zero)
            for k in range(0, 6, 2):
                span = slice(k * size, (k + 2) * size)
                even = jnp.where(low, pairs[k], turned[k + 1])
                odd = jnp.where(low, turned[k], pairs[k + 1])
                tiles[i * bc + j, :half, span] = even.astype(BF16)
                tiles[i * bc + j, half:, span] = odd.astype(BF16)

    fetches[5].wait()
    blocks_loop(br, arrange, 2)

    wait_halo(inputs[0], 0, (0,))
    for side, inside in enumerate((rx > 0, rx < n - 1)):
        values = gate(halo_rows[2, side].reshape(bc * size, feats))
        kept = values * jnp.where(inside, 1.0, 0.0).astype(BF16)
        halo_rows[0, side] = kept.reshape(bc, size, feats)
    wait_halo(gated, 0, (1,))
    near(gated, 0)

    def wait_target(k):
        source = lax.rem(rx + n - k - 1, n)
        target_copy(source, source).wait_recv()

    each(n - 1, wait_target)
    spot = lax.broadcasted_iota(jnp.int32, (size, CAP * size), 1) % size
    row = lax.broadcasted_iota(jnp.int32, (size, CAP * size), 0)
    unit = jnp.where(row == 2 * (spot % half) + spot // half, 1.0, 0.0).astype(BF16)
    for source in range(n):
        named = target_recv[source, 0:1]
        span = slice(source % 2 * CAP * size, (source % 2 + 1) * CAP * size)
        for block in range(blocks):
            hit = jnp.where(named == float(block), 1.0, 0.0).astype(BF16)
            select[source // 2, block * size : (block + 1) * size, span] = unit * hit

    strip = bc * size

    def end_first(i, total):
        first[i] = total.astype(BF16).reshape(bc, size, feats)
        if i == br - 1:
            start_halo(first, 1, (0,))

    add_far(0, end_first)
    start_halo(first, 1, (1,))
    send_group(first, 1, 0, False, False)
    send_rest(first, 1)

    for k in (10, 11):
        fetches[k].wait()
    for t in range(steps):
        span = slice(t * channels, (t + 1) * channels)
        for hop in range(3):
            at = (2 + hop) * feats + t * channels
            table[span, at : at + channels] = w_mix[hop].astype(F32)
        bias_table[2:3, span] = bias_mix[...]
    mixes = [table[:, (2 + h) * feats : (3 + h) * feats].astype(BF16) for h in range(3)]
    early_mix = jnp.concatenate(mixes[:2], axis=0)
    late_mix = jnp.concatenate([mixes[2], mixes[2]], axis=0)

    for i in range(br):
        known = [gated[i].reshape(strip, feats), first[i].reshape(strip, feats)]
        own = dot(jnp.concatenate(known, axis=1), early_mix) + bias_table[2:3]
        base[i * strip : (i + 1) * strip] = own + cell[i].reshape(strip, feats).astype(F32)
    wait_halo(first, 1)
    near(first, 1)

    def end_second(i, second):
        upper = second.astype(BF16)
        lower = (second - upper.astype(F32)).astype(BF16)
        total = base[i * strip : (i + 1) * strip]
        total = total + dot(jnp.concatenate([upper, lower], axis=1), late_mix)
        out[i] = total.astype(BF16).reshape(bc, size, feats)

    add_far(1, end_second)

    for hop, signals in enumerate(((inputs[0], gated), (first, first))):
        for which in range(2):
            for sends, gets, copy in halo_copies(signals[which], hop)[2 * which : 2 * which + 2]:
                pl.when(sends)(copy.wait_send)

        def sent(k):
            d = destination(k)
            far_copy(hop, d, rx).wait_send()
            if hop == 0:
                target_copy(d, rx).wait_send()

        each(n - 1, sent)


def local(
    n,
    ny,
    cell_input,
    w_filter,
    w_gate,
    bias_filter,
    bias_gate,
    adjacency,
    out_block,
    out_dev,
    out_target,
    out_tiles,
    w_mix,
    bias_mix,
):
    br, bc, size, feats = cell_input.shape
    blocks = br * bc
    rows = blocks * size
    edges = out_tiles.shape[2]
    channels = w_filter.shape[1]
    half = size // 2
    stride = -(-edges // 8) * 8
    assert feats == 128 and size == 64 and br == bc == 4 and n % 4 == 0
    vmem = pl.BlockSpec(memory_space=pltpu.VMEM)
    dma = pltpu.SemaphoreType.DMA
    hbm = pl.BlockSpec(memory_space=pltpu.HBM)
    operands = (
        cell_input,
        w_filter,
        w_gate,
        bias_filter.reshape(1, channels),
        bias_gate.reshape(1, channels),
        adjacency.transpose(0, 2, 1, 3),
        out_block,
        out_dev.reshape(out_block.shape),
        out_target,
        out_tiles,
        w_mix,
        bias_mix.reshape(1, channels),
    )
    scratch = [
        (pltpu.SMEM if k in (6, 7, 8) else pltpu.VMEM)(a.shape, a.dtype)
        for k, a in enumerate(operands)
    ] + [
        pltpu.VMEM((br, bc, size, feats), BF16),
        pltpu.VMEM((br, bc, size, feats), BF16),
        pltpu.VMEM((3, 2, bc, size, feats), BF16),
        pltpu.VMEM((2, 2, br, size, feats), BF16),
        pltpu.VMEM((2, n, CAP * size, feats), BF16),
        pltpu.VMEM((2, n, CAP * size, feats), BF16),
        pltpu.VMEM((n, 1, CAP * size), F32),
        pltpu.VMEM((n, 1, CAP * size), F32),
        pltpu.VMEM((n // 2, rows, 2 * CAP * size), BF16),
        pltpu.VMEM((blocks, size, 6 * size), BF16),
        pltpu.VMEM((edges, size, 2 * size), BF16),
        pltpu.VMEM((2, 3, half * 8, 2 * size), F32),
        pltpu.VMEM((half * stride, 2 * size), F32),
        pltpu.VMEM((feats, 5 * feats), F32),
        pltpu.VMEM((8, feats), F32),
        pltpu.VMEM((rows, feats), F32),
        pltpu.VMEM((rows, feats), F32),
        dma((2, n)),
        dma((2, n)),
        dma((n,)),
        dma((n,)),
        dma((2, 2, 2)),
        dma((2, 2, 2)),
        dma((12,)),
        pltpu.SMEM((n, 3 * CAP), jnp.int32),
    ]
    near_flops = 2 * 2 * 5 * rows * size * feats
    return pl.pallas_call(
        functools.partial(kernel, n, ny),
        out_shape=jax.ShapeDtypeStruct(cell_input.shape, BF16),
        in_specs=[hbm] * 12,
        out_specs=vmem,
        scratch_shapes=scratch,
        cost_estimate=pl.CostEstimate(
            flops=near_flops, bytes_accessed=2 * rows * feats * 2, transcendentals=2 * rows * feats
        ),
        compiler_params=pltpu.CompilerParams(
            collective_id=0, has_side_effects=True, vmem_limit_bytes=40 * 1024 * 1024
        ),
    )(*(pltpu.with_memory_space_constraint(a, pltpu.HBM) for a in operands))


def solution(mesh):
    in_specs = (
        P("rx", "ry", None, None),
        P(),
        P(),
        P(),
        P(),
        P("rx", "ry", None, None),
        P("rx", "ry", None),
        P("rx", "ry", None, None),
        P("rx", "ry", None),
        P("rx", "ry", None, None),
        P(),
        P(),
    )
    out_specs = P("rx", "ry", None, None)
    body = functools.partial(local, mesh.shape["rx"], mesh.shape["ry"])
    return jax.shard_map(body, mesh=mesh, in_specs=in_specs, out_specs=out_specs, check_vma=False)
```

```python
import functools

import jax
import jax.numpy as jnp
from jax import lax
from jax.experimental import pallas as pl
from jax.experimental.pallas import tpu as pltpu
from jax.sharding import PartitionSpec as P

DILATION_STEP = 2
CAP = 2
MESH = pl.DeviceIdType.MESH
F32 = jnp.float32
BF16 = jnp.bfloat16


def dot(a, b):
    return jnp.dot(a, b, preferred_element_type=F32)


def each(count, body, limit=8):
    if count <= limit:
        for k in range(count):
            body(k)
    else:

        def step(k, carry):
            body(k)
            return carry

        lax.fori_loop(0, count, step, 0)


def blocks_loop(count, body, unroll):
    def step(k, carry):
        body(k)
        return carry

    lax.fori_loop(0, count, step, 0, unroll=unroll)


def kernel(
    n,
    ny,
    *refs,
):
    inputs, (out, *landing), refs = refs[:12], refs[12:25], refs[25:]
    (
        cell,
        w_filter,
        w_gate,
        bias_filter,
        bias_gate,
        adjacency,
        out_block,
        out_dev,
        out_target,
        out_tiles,
        w_mix,
        bias_mix,
    ) = landing
    (
    gated,
    first,
    halo_rows,
    halo_cols,
    send_buf,
    recv_buf,
    target_send,
    target_recv,
    select,
    tiles,
    edge_tiles,
    spread,
    edge_spread,
    table,
    bias_table,
    acc,
    base,
    send_sem,
    recv_sem,
    target_send_sem,
    target_recv_sem,
    halo_send_sem,
    halo_recv_sem,
    fetch_sem,
    route,
    ) = refs
    fetches = [
        pltpu.make_async_copy(src, dst, fetch_sem.at[k])
        for k, (src, dst) in enumerate(zip(inputs, landing))
    ]
    for k in (6, 7, 8, 1, 2, 3, 4, 9, 0, 10, 11, 5):
        fetches[k].start()
    br, bc, size, feats = cell.shape
    blocks = br * bc
    rows = blocks * size
    half = size // 2
    edges = out_tiles.shape[2]
    channels = w_filter.shape[1]
    steps = feats // channels
    stride = edge_spread.shape[0] // half
    rx = lax.axis_index("rx")
    ry = lax.axis_index("ry")

    barrier = pltpu.get_barrier_semaphore()

    def greet(k):
        pl.semaphore_signal(
            barrier, inc=1, device_id={"rx": lax.rem(rx + k + 1, n)}, device_id_type=MESH
        )

    each(n - 1, greet)

    @pl.when(ry > 0)
    def _():
        pl.semaphore_signal(barrier, inc=1, device_id={"ry": ry - 1}, device_id_type=MESH)

    @pl.when(ry < ny - 1)
    def _():
        pl.semaphore_signal(barrier, inc=1, device_id={"ry": ry + 1}, device_id_type=MESH)

    def halo_copies(signal, hop):
        sides = []
        for which, (axis, here, count, halo) in enumerate(
            (("rx", rx, n, halo_rows), ("ry", ry, ny, halo_cols))
        ):
            last = (br if which == 0 else bc) - 1
            for side, (edge, step) in enumerate(((last, 1), (0, -1))):
                src = signal.at[edge] if which == 0 else signal.at[:, edge]
                copy = pltpu.make_async_remote_copy(
                    src_ref=src,
                    dst_ref=halo.at[2 - hop if which == 0 else hop, side],
                    send_sem=halo_send_sem.at[hop, which, side],
                    recv_sem=halo_recv_sem.at[hop, which, side],
                    device_id={axis: jnp.clip(here + step, 0, count - 1)},
                    device_id_type=MESH,
                )
                sends = (here < count - 1) if step == 1 else (here > 0)
                gets = (here > 0) if step == 1 else (here < count - 1)
                sides.append((sends, gets, copy))
        return sides

    def start_halo(signal, hop, axes=(0, 1)):
        for which in axes:
            for sends, gets, copy in halo_copies(signal, hop)[2 * which : 2 * which + 2]:
                pl.when(sends)(copy.start)

    def wait_halo(signal, hop, axes=(0, 1)):
        for which in axes:
            for sends, gets, copy in halo_copies(signal, hop)[2 * which : 2 * which + 2]:
                pl.when(gets)(copy.wait_recv)

    pl.semaphore_wait(
        barrier,
        n - 1 + jnp.where(ry > 0, 1, 0) + jnp.where(ry < ny - 1, 1, 0),
    )

    zero_side = jnp.zeros((2,) + halo_rows.shape[2:], BF16)

    @pl.when(rx == 0)
    def _():
        halo_rows[1:, 0] = zero_side

    @pl.when(rx == n - 1)
    def _():
        halo_rows[1:, 1] = zero_side

    @pl.when(ry == 0)
    def _():
        halo_cols[:, 0] = zero_side

    @pl.when(ry == ny - 1)
    def _():
        halo_cols[:, 1] = zero_side

    start_halo(inputs[0], 0, (0,))
    for k in range(1, 5):
        fetches[k].wait()

    table[...] = jnp.zeros_like(table)
    for t in range(steps):
        span = slice(t * channels, (t + 1) * channels)
        for which, weights in enumerate((w_filter, w_gate)):
            for tap, to in ((1, t), (0, t + DILATION_STEP)):
                if to < steps:
                    at = which * feats + to * channels
                    table[span, at : at + channels] = weights[tap].astype(F32)
        bias_table[0:1, span] = bias_filter[...]
        bias_table[1:2, span] = bias_gate[...]
    taps = table[:, : 2 * feats].astype(BF16)

    def gate(block_rows):
        pre = dot(block_rows, taps)
        pre_f = pre[:, :feats] + bias_table[0:1]
        pre_g = pre[:, feats:] + bias_table[1:2]
        value = jnp.tanh(pre_f) * (0.5 * jnp.tanh(0.5 * pre_g) + 0.5)
        return value.astype(BF16)

    for k in range(6, 10):
        fetches[k].wait()

    for r in range(half):
        piece = out_tiles[0, 0, :, r * 2 * size : (r + 1) * 2 * size]
        edge_spread[r * stride : r * stride + edges] = piece.astype(F32)
    for e in range(edges):
        pairs = edge_spread[pl.ds(e, half, stride=stride), :]
        edge_tiles[e, :half] = pairs.astype(BF16)
        edge_tiles[e, half:] = pltpu.roll(pairs, size, 1).astype(BF16)

    part = n // 2

    def destination(k):
        side = (rx // part + 1 + k // part) % 2
        return side * part + (rx % part + k % part + 1) % part

    lane = lax.broadcasted_iota(jnp.int32, (1, CAP * size), 1)

    def far_copy(hop, d, source):
        return pltpu.make_async_remote_copy(
            src_ref=send_buf.at[hop, d],
            dst_ref=recv_buf.at[hop, source],
            send_sem=send_sem.at[hop, d],
            recv_sem=recv_sem.at[hop, source],
            device_id={"rx": d},
            device_id_type=MESH,
        )

    def target_copy(d, source):
        return pltpu.make_async_remote_copy(
            src_ref=target_send.at[d],
            dst_ref=target_recv.at[source],
            send_sem=target_send_sem.at[d],
            recv_sem=target_recv_sem.at[source],
            device_id={"rx": d},
            device_id_type=MESH,
        )

    def find_route(k):
        d = destination(k)
        head, tail = jnp.int32(-1), jnp.int32(-1)
        for e in range(edges):
            hit = out_dev[0, 0, e] == d
            head = jnp.where(hit & (head < 0), e, head)
            tail = jnp.where(hit, e, tail)
        found = ((head, head >= 0), (tail, tail != head))
        for c, (index, valid) in enumerate(found):
            index = jnp.maximum(index, 0)
            route[k, c] = index
            route[k, CAP + c] = out_block[0, 0, index]
            route[k, 2 * CAP + c] = jnp.where(valid, 1, 0)

    def send_targets(k, own):
        d = destination(k)
        names = [
            jnp.where(route[k, 2 * CAP + c] == 1, out_target[0, 0, route[k, c]], -1)
            for c in range(CAP)
        ]
        named = jnp.where(lane < size, names[0], names[1]).astype(F32)
        if own:
            target_recv[rx] = named
        else:
            target_send[d] = named
            target_copy(d, rx).start()

    team = 4

    def send_group(signal, hop, start, last):
        ks = [start + g for g in range(team)]
        picked = []
        for k in ks:
            for c in range(CAP):
                b = route[k, CAP + c]
                picked.append(signal[lax.div(b, bc), lax.rem(b, bc)])
        sums = []
        for g, k in enumerate(ks):
            for c in range(CAP):
                product = dot(edge_tiles[route[k, c]][:, :size], picked[g * CAP + c])
                sums.append((product * route[k, 2 * CAP + c].astype(F32)).astype(BF16))
        for g, k in enumerate(ks):
            both = jnp.concatenate(sums[g * CAP : (g + 1) * CAP], axis=0)
            if last and g == team - 1:
                recv_buf[hop, rx] = both
            else:
                send_buf[hop, destination(k)] = both
        for g, k in enumerate(ks):
            if not (last and g == team - 1):
                far_copy(hop, destination(k), rx).start()

    def send_far(signal, hop):
        each(n // team - 1, lambda g: send_group(signal, hop, g * team, False))
        send_group(signal, hop, n - team, True)

    part_pairs = n // 4

    def add_far(hop, finish):
        strip = bc * size

        def wait_source(source):
            far_copy(hop, source, source).wait_recv()

        def one(q):
            side = (rx // part + q // part_pairs) % 2
            pair = side * part_pairs + (rx % part // 2 + q % part_pairs) % part_pairs
            if isinstance(q, int) and q == 0:
                wait_source(rx + 1 - 2 * (rx % 2))
            else:
                wait_source(2 * pair)
                wait_source(2 * pair + 1)
            landed = recv_buf[hop, pl.ds(2 * pair, 2)].reshape(2 * CAP * size, feats)
            for i in (0, br - 1, *range(1, br - 1)):
                span = slice(i * strip, (i + 1) * strip)
                total = acc[span] + dot(select[pair, span], landed)
                if isinstance(q, int) and q == n // 2 - 1:
                    finish(i, total)
                else:
                    acc[span] = total

        one(0)
        each(n // 2 - 2, lambda q: one(q + 1))
        one(n // 2 - 1)

    def near(signal, hop):
        for i in range(br):
            for j in range(bc):
                up = signal[i - 1, j] if i > 0 else halo_rows[hop, 0, j]
                down = signal[i + 1, j] if i < br - 1 else halo_rows[hop, 1, j]
                left = signal[i, j - 1] if j > 0 else halo_cols[hop, 0, i]
                right = signal[i, j + 1] if j < bc - 1 else halo_cols[hop, 1, i]
                column = jnp.concatenate([signal[i, j], up, down, left, right], axis=0)
                total = dot(tiles[i * bc + j][:, : 5 * size], column)
                at = (i * bc + j) * size
                acc[pl.ds(at, half, stride=2), :] = total[:half]
                acc[pl.ds(at + 1, half, stride=2), :] = total[half:]

    each(n, find_route)
    each(n - 1, lambda k: send_targets(k, False))
    send_targets(n - 1, True)
    fetches[0].wait()
    for i in range(br):
        gated[i] = gate(cell[i].reshape(bc * size, feats)).reshape(bc, size, feats)
    start_halo(gated, 0, (1,))
    send_far(gated, 0)

    low = lax.broadcasted_iota(jnp.int32, (half, 2 * size), 1) < size

    def arrange(i):
        slot = lax.rem(i, spread.shape[0])
        for k in range(5):
            for r in range(half):
                piece = adjacency[i, k, :, r * 2 * size : (r + 1) * 2 * size]
                at = r * 8 + k % 2 * bc
                spread[slot, k // 2, at : at + bc] = piece.astype(F32)
        for j in range(bc):
            pairs = [
                spread[slot, k // 2, pl.ds(k % 2 * bc + j, half, stride=8), :] for k in range(5)
            ]
            turned = [pltpu.roll(pair, size, 1) for pair in pairs]
            zero = jnp.zeros_like(pairs[0])
            pairs.append(zero)
            turned.append(zero)
            for k in range(0, 6, 2):
                span = slice(k * size, (k + 2) * size)
                even = jnp.where(low, pairs[k], turned[k + 1])
                odd = jnp.where(low, turned[k], pairs[k + 1])
                tiles[i * bc + j, :half, span] = even.astype(BF16)
                tiles[i * bc + j, half:, span] = odd.astype(BF16)

    fetches[5].wait()
    blocks_loop(br, arrange, 2)

    wait_halo(inputs[0], 0, (0,))
    for side, inside in enumerate((rx > 0, rx < n - 1)):
        values = gate(halo_rows[2, side].reshape(bc * size, feats))
        kept = values * jnp.where(inside, 1.0, 0.0).astype(BF16)
        halo_rows[0, side] = kept.reshape(bc, size, feats)
    wait_halo(gated, 0, (1,))
    near(gated, 0)

    def wait_target(k):
        source = lax.rem(rx + n - k - 1, n)
        target_copy(source, source).wait_recv()

    each(n - 1, wait_target)
    spot = lax.broadcasted_iota(jnp.int32, (size, CAP * size), 1) % size
    row = lax.broadcasted_iota(jnp.int32, (size, CAP * size), 0)
    unit = jnp.where(row == 2 * (spot % half) + spot // half, 1.0, 0.0).astype(BF16)
    for source in range(n):
        named = target_recv[source, 0:1]
        span = slice(source % 2 * CAP * size, (source % 2 + 1) * CAP * size)
        for block in range(blocks):
            hit = jnp.where(named == float(block), 1.0, 0.0).astype(BF16)
            select[source // 2, block * size : (block + 1) * size, span] = unit * hit

    strip = bc * size

    def end_first(i, total):
        first[i] = total.astype(BF16).reshape(bc, size, feats)
        if i == br - 1:
            start_halo(first, 1, (0,))

    add_far(0, end_first)
    start_halo(first, 1, (1,))
    send_far(first, 1)

    for k in (10, 11):
        fetches[k].wait()
    for t in range(steps):
        span = slice(t * channels, (t + 1) * channels)
        for hop in range(3):
            at = (2 + hop) * feats + t * channels
            table[span, at : at + channels] = w_mix[hop].astype(F32)
        bias_table[2:3, span] = bias_mix[...]
    mixes = [table[:, (2 + h) * feats : (3 + h) * feats].astype(BF16) for h in range(3)]
    early_mix = jnp.concatenate(mixes[:2], axis=0)
    late_mix = jnp.concatenate([mixes[2], mixes[2]], axis=0)

    for i in range(br):
        known = [gated[i].reshape(strip, feats), first[i].reshape(strip, feats)]
        own = dot(jnp.concatenate(known, axis=1), early_mix) + bias_table[2:3]
        base[i * strip : (i + 1) * strip] = own + cell[i].reshape(strip, feats).astype(F32)
    wait_halo(first, 1)
    near(first, 1)

    def end_second(i, second):
        upper = second.astype(BF16)
        lower = (second - upper.astype(F32)).astype(BF16)
        total = base[i * strip : (i + 1) * strip]
        total = total + dot(jnp.concatenate([upper, lower], axis=1), late_mix)
        out[i] = total.astype(BF16).reshape(bc, size, feats)

    add_far(1, end_second)

    for hop, signals in enumerate(((inputs[0], gated), (first, first))):
        for which in range(2):
            for sends, gets, copy in halo_copies(signals[which], hop)[2 * which : 2 * which + 2]:
                pl.when(sends)(copy.wait_send)

        def sent(k):
            d = destination(k)
            far_copy(hop, d, rx).wait_send()
            if hop == 0:
                target_copy(d, rx).wait_send()

        each(n - 1, sent)


def local(
    n,
    ny,
    cell_input,
    w_filter,
    w_gate,
    bias_filter,
    bias_gate,
    adjacency,
    out_block,
    out_dev,
    out_target,
    out_tiles,
    w_mix,
    bias_mix,
):
    br, bc, size, feats = cell_input.shape
    blocks = br * bc
    rows = blocks * size
    edges = out_tiles.shape[2]
    channels = w_filter.shape[1]
    half = size // 2
    stride = -(-edges // 8) * 8
    assert feats == 128 and size == 64 and br == bc == 4 and n % 4 == 0
    vmem = pl.BlockSpec(memory_space=pltpu.VMEM)
    dma = pltpu.SemaphoreType.DMA
    hbm = pl.BlockSpec(memory_space=pltpu.HBM)
    operands = (
        cell_input,
        w_filter,
        w_gate,
        bias_filter.reshape(1, channels),
        bias_gate.reshape(1, channels),
        adjacency.transpose(0, 2, 1, 3),
        out_block,
        out_dev.reshape(out_block.shape),
        out_target,
        out_tiles,
        w_mix,
        bias_mix.reshape(1, channels),
    )
    scratch = [
        (pltpu.SMEM if k in (6, 7, 8) else pltpu.VMEM)(a.shape, a.dtype)
        for k, a in enumerate(operands)
    ] + [
        pltpu.VMEM((br, bc, size, feats), BF16),
        pltpu.VMEM((br, bc, size, feats), BF16),
        pltpu.VMEM((3, 2, bc, size, feats), BF16),
        pltpu.VMEM((2, 2, br, size, feats), BF16),
        pltpu.VMEM((2, n, CAP * size, feats), BF16),
        pltpu.VMEM((2, n, CAP * size, feats), BF16),
        pltpu.VMEM((n, 1, CAP * size), F32),
        pltpu.VMEM((n, 1, CAP * size), F32),
        pltpu.VMEM((n // 2, rows, 2 * CAP * size), BF16),
        pltpu.VMEM((blocks, size, 6 * size), BF16),
        pltpu.VMEM((edges, size, 2 * size), BF16),
        pltpu.VMEM((2, 3, half * 8, 2 * size), F32),
        pltpu.VMEM((half * stride, 2 * size), F32),
        pltpu.VMEM((feats, 5 * feats), F32),
        pltpu.VMEM((8, feats), F32),
        pltpu.VMEM((rows, feats), F32),
        pltpu.VMEM((rows, feats), F32),
        dma((2, n)),
        dma((2, n)),
        dma((n,)),
        dma((n,)),
        dma((2, 2, 2)),
        dma((2, 2, 2)),
        dma((12,)),
        pltpu.SMEM((n, 3 * CAP), jnp.int32),
    ]
    near_flops = 2 * 2 * 5 * rows * size * feats
    return pl.pallas_call(
        functools.partial(kernel, n, ny),
        out_shape=jax.ShapeDtypeStruct(cell_input.shape, BF16),
        in_specs=[hbm] * 12,
        out_specs=vmem,
        scratch_shapes=scratch,
        cost_estimate=pl.CostEstimate(
            flops=near_flops, bytes_accessed=2 * rows * feats * 2, transcendentals=2 * rows * feats
        ),
        compiler_params=pltpu.CompilerParams(
            collective_id=0, has_side_effects=True, vmem_limit_bytes=40 * 1024 * 1024
        ),
    )(*(pltpu.with_memory_space_constraint(a, pltpu.HBM) for a in operands))


def solution(mesh):
    in_specs = (
        P("rx", "ry", None, None),
        P(),
        P(),
        P(),
        P(),
        P("rx", "ry", None, None),
        P("rx", "ry", None),
        P("rx", "ry", None, None),
        P("rx", "ry", None),
        P("rx", "ry", None, None),
        P(),
        P(),
    )
    out_specs = P("rx", "ry", None, None)
    body = functools.partial(local, mesh.shape["rx"], mesh.shape["ry"])
    return jax.shard_map(body, mesh=mesh, in_specs=in_specs, out_specs=out_specs, check_vma=False)
```

```python
import functools

import jax
import jax.numpy as jnp
from jax import lax
from jax.experimental import pallas as pl
from jax.experimental.pallas import tpu as pltpu
from jax.sharding import PartitionSpec as P

DILATION_STEP = 2
CAP = 2
MESH = pl.DeviceIdType.MESH
F32 = jnp.float32
BF16 = jnp.bfloat16


def dot(a, b):
    return jnp.dot(a, b, preferred_element_type=F32)


def each(count, body, limit=8):
    if count <= limit:
        for k in range(count):
            body(k)
    else:

        def step(k, carry):
            body(k)
            return carry

        lax.fori_loop(0, count, step, 0)


def blocks_loop(count, body, unroll):
    def step(k, carry):
        body(k)
        return carry

    lax.fori_loop(0, count, step, 0, unroll=unroll)


def kernel(
    n,
    ny,
    *refs,
):
    inputs, (out, *landing), refs = refs[:12], refs[12:25], refs[25:]
    (
        cell,
        w_filter,
        w_gate,
        bias_filter,
        bias_gate,
        adjacency,
        out_block,
        out_dev,
        out_target,
        out_tiles,
        w_mix,
        bias_mix,
    ) = landing
    (
    gated,
    first,
    halo_rows,
    halo_cols,
    send_buf,
    recv_buf,
    target_send,
    target_recv,
    select,
    tiles,
    edge_tiles,
    spread,
    edge_spread,
    table,
    bias_table,
    acc,
    base,
    send_sem,
    recv_sem,
    target_send_sem,
    target_recv_sem,
    halo_send_sem,
    halo_recv_sem,
    fetch_sem,
    route,
    ) = refs
    fetches = [
        pltpu.make_async_copy(src, dst, fetch_sem.at[k])
        for k, (src, dst) in enumerate(zip(inputs, landing))
    ]
    for k in (6, 7, 8, 1, 2, 3, 4, 9, 0, 10, 11, 5):
        fetches[k].start()
    br, bc, size, feats = cell.shape
    blocks = br * bc
    rows = blocks * size
    half = size // 2
    edges = out_tiles.shape[2]
    channels = w_filter.shape[1]
    steps = feats // channels
    stride = edge_spread.shape[0] // half
    rx = lax.axis_index("rx")
    ry = lax.axis_index("ry")

    barrier = pltpu.get_barrier_semaphore()

    def greet(k):
        pl.semaphore_signal(
            barrier, inc=1, device_id={"rx": lax.rem(rx + k + 1, n)}, device_id_type=MESH
        )

    each(n - 1, greet)

    @pl.when(ry > 0)
    def _():
        pl.semaphore_signal(barrier, inc=1, device_id={"ry": ry - 1}, device_id_type=MESH)

    @pl.when(ry < ny - 1)
    def _():
        pl.semaphore_signal(barrier, inc=1, device_id={"ry": ry + 1}, device_id_type=MESH)

    def halo_copies(signal, hop):
        sides = []
        for which, (axis, here, count, halo) in enumerate(
            (("rx", rx, n, halo_rows), ("ry", ry, ny, halo_cols))
        ):
            last = (br if which == 0 else bc) - 1
            for side, (edge, step) in enumerate(((last, 1), (0, -1))):
                src = signal.at[edge] if which == 0 else signal.at[:, edge]
                copy = pltpu.make_async_remote_copy(
                    src_ref=src,
                    dst_ref=halo.at[2 - hop if which == 0 else hop, side],
                    send_sem=halo_send_sem.at[hop, which, side],
                    recv_sem=halo_recv_sem.at[hop, which, side],
                    device_id={axis: jnp.clip(here + step, 0, count - 1)},
                    device_id_type=MESH,
                )
                sends = (here < count - 1) if step == 1 else (here > 0)
                gets = (here > 0) if step == 1 else (here < count - 1)
                sides.append((sends, gets, copy))
        return sides

    def start_halo(signal, hop, axes=(0, 1)):
        for which in axes:
            for sends, gets, copy in halo_copies(signal, hop)[2 * which : 2 * which + 2]:
                pl.when(sends)(copy.start)

    def wait_halo(signal, hop, axes=(0, 1)):
        for which in axes:
            for sends, gets, copy in halo_copies(signal, hop)[2 * which : 2 * which + 2]:
                pl.when(gets)(copy.wait_recv)

    pl.semaphore_wait(
        barrier,
        n - 1 + jnp.where(ry > 0, 1, 0) + jnp.where(ry < ny - 1, 1, 0),
    )

    zero_side = jnp.zeros((2,) + halo_rows.shape[2:], BF16)

    @pl.when(rx == 0)
    def _():
        halo_rows[1:, 0] = zero_side

    @pl.when(rx == n - 1)
    def _():
        halo_rows[1:, 1] = zero_side

    @pl.when(ry == 0)
    def _():
        halo_cols[:, 0] = zero_side

    @pl.when(ry == ny - 1)
    def _():
        halo_cols[:, 1] = zero_side

    start_halo(inputs[0], 0, (0,))
    for k in range(1, 5):
        fetches[k].wait()

    table[...] = jnp.zeros_like(table)
    for t in range(steps):
        span = slice(t * channels, (t + 1) * channels)
        for which, weights in enumerate((w_filter, w_gate)):
            for tap, to in ((1, t), (0, t + DILATION_STEP)):
                if to < steps:
                    at = which * feats + to * channels
                    table[span, at : at + channels] = weights[tap].astype(F32)
        bias_table[0:1, span] = bias_filter[...]
        bias_table[1:2, span] = bias_gate[...]
    taps = table[:, : 2 * feats].astype(BF16)

    def gate(block_rows):
        pre = dot(block_rows, taps)
        pre_f = pre[:, :feats] + bias_table[0:1]
        pre_g = pre[:, feats:] + bias_table[1:2]
        value = jnp.tanh(pre_f) * (0.5 * jnp.tanh(0.5 * pre_g) + 0.5)
        return value.astype(BF16)

    for k in range(6, 10):
        fetches[k].wait()

    for r in range(half):
        piece = out_tiles[0, 0, :, r * 2 * size : (r + 1) * 2 * size]
        edge_spread[r * stride : r * stride + edges] = piece.astype(F32)
    for e in range(edges):
        pairs = edge_spread[pl.ds(e, half, stride=stride), :]
        edge_tiles[e, :half] = pairs.astype(BF16)
        edge_tiles[e, half:] = pltpu.roll(pairs, size, 1).astype(BF16)

    part = n // 2

    def destination(k):
        side = (rx // part + 1 + k % 2) % 2
        return side * part + (rx % part + k // 2 + 1) % part

    lane = lax.broadcasted_iota(jnp.int32, (1, CAP * size), 1)

    def far_copy(hop, d, source):
        return pltpu.make_async_remote_copy(
            src_ref=send_buf.at[hop, d],
            dst_ref=recv_buf.at[hop, source],
            send_sem=send_sem.at[hop, d],
            recv_sem=recv_sem.at[hop, source],
            device_id={"rx": d},
            device_id_type=MESH,
        )

    def target_copy(d, source):
        return pltpu.make_async_remote_copy(
            src_ref=target_send.at[d],
            dst_ref=target_recv.at[source],
            send_sem=target_send_sem.at[d],
            recv_sem=target_recv_sem.at[source],
            device_id={"rx": d},
            device_id_type=MESH,
        )

    def find_route(k):
        d = destination(k)
        head, tail = jnp.int32(-1), jnp.int32(-1)
        for e in range(edges):
            hit = out_dev[0, 0, e] == d
            head = jnp.where(hit & (head < 0), e, head)
            tail = jnp.where(hit, e, tail)
        found = ((head, head >= 0), (tail, tail != head))
        for c, (index, valid) in enumerate(found):
            index = jnp.maximum(index, 0)
            route[k, c] = index
            route[k, CAP + c] = out_block[0, 0, index]
            route[k, 2 * CAP + c] = jnp.where(valid, 1, 0)

    def send_targets(k, own):
        d = destination(k)
        names = [
            jnp.where(route[k, 2 * CAP + c] == 1, out_target[0, 0, route[k, c]], -1)
            for c in range(CAP)
        ]
        named = jnp.where(lane < size, names[0], names[1]).astype(F32)
        if own:
            target_recv[rx] = named
        else:
            target_send[d] = named
            target_copy(d, rx).start()

    team = 4

    def send_group(signal, hop, start, last):
        ks = [start + g for g in range(team)]
        picked = []
        for k in ks:
            for c in range(CAP):
                b = route[k, CAP + c]
                picked.append(signal[lax.div(b, bc), lax.rem(b, bc)])
        sums = []
        for g, k in enumerate(ks):
            for c in range(CAP):
                product = dot(edge_tiles[route[k, c]][:, :size], picked[g * CAP + c])
                sums.append((product * route[k, 2 * CAP + c].astype(F32)).astype(BF16))
        for g, k in enumerate(ks):
            both = jnp.concatenate(sums[g * CAP : (g + 1) * CAP], axis=0)
            if last and g == team - 1:
                recv_buf[hop, rx] = both
            else:
                send_buf[hop, destination(k)] = both
        for g, k in enumerate(ks):
            if not (last and g == team - 1):
                far_copy(hop, destination(k), rx).start()

    def send_far(signal, hop):
        each(n // team - 1, lambda g: send_group(signal, hop, g * team, False))
        send_group(signal, hop, n - team, True)

    part_pairs = n // 4

    def add_far(hop, finish):
        strip = bc * size

        def wait_source(source):
            far_copy(hop, source, source).wait_recv()

        def one(q):
            side = (rx // part + q // part_pairs) % 2
            pair = side * part_pairs + (rx % part // 2 + q % part_pairs) % part_pairs
            if isinstance(q, int) and q == 0:
                wait_source(rx + 1 - 2 * (rx % 2))
            else:
                wait_source(2 * pair)
                wait_source(2 * pair + 1)
            landed = recv_buf[hop, pl.ds(2 * pair, 2)].reshape(2 * CAP * size, feats)
            for i in (0, br - 1, *range(1, br - 1)):
                span = slice(i * strip, (i + 1) * strip)
                total = acc[span] + dot(select[pair, span], landed)
                if isinstance(q, int) and q == n // 2 - 1:
                    finish(i, total)
                else:
                    acc[span] = total

        one(0)
        each(n // 2 - 2, lambda q: one(q + 1))
        one(n // 2 - 1)

    def near(signal, hop):
        for i in range(br):
            for j in range(bc):
                up = signal[i - 1, j] if i > 0 else halo_rows[hop, 0, j]
                down = signal[i + 1, j] if i < br - 1 else halo_rows[hop, 1, j]
                left = signal[i, j - 1] if j > 0 else halo_cols[hop, 0, i]
                right = signal[i, j + 1] if j < bc - 1 else halo_cols[hop, 1, i]
                column = jnp.concatenate([signal[i, j], up, down, left, right], axis=0)
                total = dot(tiles[i * bc + j][:, : 5 * size], column)
                at = (i * bc + j) * size
                acc[pl.ds(at, half, stride=2), :] = total[:half]
                acc[pl.ds(at + 1, half, stride=2), :] = total[half:]

    each(n, find_route)
    each(n - 1, lambda k: send_targets(k, False))
    send_targets(n - 1, True)
    fetches[0].wait()
    for i in range(br):
        gated[i] = gate(cell[i].reshape(bc * size, feats)).reshape(bc, size, feats)
    start_halo(gated, 0, (1,))
    send_far(gated, 0)

    low = lax.broadcasted_iota(jnp.int32, (half, 2 * size), 1) < size

    def arrange(i):
        slot = lax.rem(i, spread.shape[0])
        for k in range(5):
            for r in range(half):
                piece = adjacency[i, k, :, r * 2 * size : (r + 1) * 2 * size]
                at = r * 8 + k % 2 * bc
                spread[slot, k // 2, at : at + bc] = piece.astype(F32)
        for j in range(bc):
            pairs = [
                spread[slot, k // 2, pl.ds(k % 2 * bc + j, half, stride=8), :] for k in range(5)
            ]
            turned = [pltpu.roll(pair, size, 1) for pair in pairs]
            zero = jnp.zeros_like(pairs[0])
            pairs.append(zero)
            turned.append(zero)
            for k in range(0, 6, 2):
                span = slice(k * size, (k + 2) * size)
                even = jnp.where(low, pairs[k], turned[k + 1])
                odd = jnp.where(low, turned[k], pairs[k + 1])
                tiles[i * bc + j, :half, span] = even.astype(BF16)
                tiles[i * bc + j, half:, span] = odd.astype(BF16)

    fetches[5].wait()
    blocks_loop(br, arrange, 2)

    wait_halo(inputs[0], 0, (0,))
    for side, inside in enumerate((rx > 0, rx < n - 1)):
        values = gate(halo_rows[2, side].reshape(bc * size, feats))
        kept = values * jnp.where(inside, 1.0, 0.0).astype(BF16)
        halo_rows[0, side] = kept.reshape(bc, size, feats)
    wait_halo(gated, 0, (1,))
    near(gated, 0)

    def wait_target(k):
        source = lax.rem(rx + n - k - 1, n)
        target_copy(source, source).wait_recv()

    each(n - 1, wait_target)
    spot = lax.broadcasted_iota(jnp.int32, (size, CAP * size), 1) % size
    row = lax.broadcasted_iota(jnp.int32, (size, CAP * size), 0)
    unit = jnp.where(row == 2 * (spot % half) + spot // half, 1.0, 0.0).astype(BF16)
    for source in range(n):
        named = target_recv[source, 0:1]
        span = slice(source % 2 * CAP * size, (source % 2 + 1) * CAP * size)
        for block in range(blocks):
            hit = jnp.where(named == float(block), 1.0, 0.0).astype(BF16)
            select[source // 2, block * size : (block + 1) * size, span] = unit * hit

    strip = bc * size

    def end_first(i, total):
        first[i] = total.astype(BF16).reshape(bc, size, feats)
        if i == br - 1:
            start_halo(first, 1, (0,))

    add_far(0, end_first)
    start_halo(first, 1, (1,))
    send_far(first, 1)

    for k in (10, 11):
        fetches[k].wait()
    for t in range(steps):
        span = slice(t * channels, (t + 1) * channels)
        for hop in range(3):
            at = (2 + hop) * feats + t * channels
            table[span, at : at + channels] = w_mix[hop].astype(F32)
        bias_table[2:3, span] = bias_mix[...]
    mixes = [table[:, (2 + h) * feats : (3 + h) * feats].astype(BF16) for h in range(3)]
    early_mix = jnp.concatenate(mixes[:2], axis=0)
    late_mix = jnp.concatenate([mixes[2], mixes[2]], axis=0)

    for i in range(br):
        known = [gated[i].reshape(strip, feats), first[i].reshape(strip, feats)]
        own = dot(jnp.concatenate(known, axis=1), early_mix) + bias_table[2:3]
        base[i * strip : (i + 1) * strip] = own + cell[i].reshape(strip, feats).astype(F32)
    wait_halo(first, 1)
    near(first, 1)

    def end_second(i, second):
        upper = second.astype(BF16)
        lower = (second - upper.astype(F32)).astype(BF16)
        total = base[i * strip : (i + 1) * strip]
        total = total + dot(jnp.concatenate([upper, lower], axis=1), late_mix)
        out[i] = total.astype(BF16).reshape(bc, size, feats)

    add_far(1, end_second)

    for hop, signals in enumerate(((inputs[0], gated), (first, first))):
        for which in range(2):
            for sends, gets, copy in halo_copies(signals[which], hop)[2 * which : 2 * which + 2]:
                pl.when(sends)(copy.wait_send)

        def sent(k):
            d = destination(k)
            far_copy(hop, d, rx).wait_send()
            if hop == 0:
                target_copy(d, rx).wait_send()

        each(n - 1, sent)


def local(
    n,
    ny,
    cell_input,
    w_filter,
    w_gate,
    bias_filter,
    bias_gate,
    adjacency,
    out_block,
    out_dev,
    out_target,
    out_tiles,
    w_mix,
    bias_mix,
):
    br, bc, size, feats = cell_input.shape
    blocks = br * bc
    rows = blocks * size
    edges = out_tiles.shape[2]
    channels = w_filter.shape[1]
    half = size // 2
    stride = -(-edges // 8) * 8
    assert feats == 128 and size == 64 and br == bc == 4 and n % 4 == 0
    vmem = pl.BlockSpec(memory_space=pltpu.VMEM)
    dma = pltpu.SemaphoreType.DMA
    hbm = pl.BlockSpec(memory_space=pltpu.HBM)
    operands = (
        cell_input,
        w_filter,
        w_gate,
        bias_filter.reshape(1, channels),
        bias_gate.reshape(1, channels),
        adjacency.transpose(0, 2, 1, 3),
        out_block,
        out_dev.reshape(out_block.shape),
        out_target,
        out_tiles,
        w_mix,
        bias_mix.reshape(1, channels),
    )
    scratch = [
        (pltpu.SMEM if k in (6, 7, 8) else pltpu.VMEM)(a.shape, a.dtype)
        for k, a in enumerate(operands)
    ] + [
        pltpu.VMEM((br, bc, size, feats), BF16),
        pltpu.VMEM((br, bc, size, feats), BF16),
        pltpu.VMEM((3, 2, bc, size, feats), BF16),
        pltpu.VMEM((2, 2, br, size, feats), BF16),
        pltpu.VMEM((2, n, CAP * size, feats), BF16),
        pltpu.VMEM((2, n, CAP * size, feats), BF16),
        pltpu.VMEM((n, 1, CAP * size), F32),
        pltpu.VMEM((n, 1, CAP * size), F32),
        pltpu.VMEM((n // 2, rows, 2 * CAP * size), BF16),
        pltpu.VMEM((blocks, size, 6 * size), BF16),
        pltpu.VMEM((edges, size, 2 * size), BF16),
        pltpu.VMEM((2, 3, half * 8, 2 * size), F32),
        pltpu.VMEM((half * stride, 2 * size), F32),
        pltpu.VMEM((feats, 5 * feats), F32),
        pltpu.VMEM((8, feats), F32),
        pltpu.VMEM((rows, feats), F32),
        pltpu.VMEM((rows, feats), F32),
        dma((2, n)),
        dma((2, n)),
        dma((n,)),
        dma((n,)),
        dma((2, 2, 2)),
        dma((2, 2, 2)),
        dma((12,)),
        pltpu.SMEM((n, 3 * CAP), jnp.int32),
    ]
    near_flops = 2 * 2 * 5 * rows * size * feats
    return pl.pallas_call(
        functools.partial(kernel, n, ny),
        out_shape=jax.ShapeDtypeStruct(cell_input.shape, BF16),
        in_specs=[hbm] * 12,
        out_specs=vmem,
        scratch_shapes=scratch,
        cost_estimate=pl.CostEstimate(
            flops=near_flops, bytes_accessed=2 * rows * feats * 2, transcendentals=2 * rows * feats
        ),
        compiler_params=pltpu.CompilerParams(
            collective_id=0, has_side_effects=True, vmem_limit_bytes=40 * 1024 * 1024
        ),
    )(*(pltpu.with_memory_space_constraint(a, pltpu.HBM) for a in operands))


def solution(mesh):
    in_specs = (
        P("rx", "ry", None, None),
        P(),
        P(),
        P(),
        P(),
        P("rx", "ry", None, None),
        P("rx", "ry", None),
        P("rx", "ry", None, None),
        P("rx", "ry", None),
        P("rx", "ry", None, None),
        P(),
        P(),
    )
    out_specs = P("rx", "ry", None, None)
    body = functools.partial(local, mesh.shape["rx"], mesh.shape["ry"])
    return jax.shard_map(body, mesh=mesh, in_specs=in_specs, out_specs=out_specs, check_vma=False)
```

```python
import functools

import jax
import jax.numpy as jnp
from jax import lax
from jax.experimental import pallas as pl
from jax.experimental.pallas import tpu as pltpu
from jax.sharding import PartitionSpec as P

DILATION_STEP = 2
CAP = 2
MESH = pl.DeviceIdType.MESH
F32 = jnp.float32
BF16 = jnp.bfloat16


def dot(a, b):
    return jnp.dot(a, b, preferred_element_type=F32)


def each(count, body, limit=8):
    if count <= limit:
        for k in range(count):
            body(k)
    else:

        def step(k, carry):
            body(k)
            return carry

        lax.fori_loop(0, count, step, 0)


def blocks_loop(count, body, unroll):
    def step(k, carry):
        body(k)
        return carry

    lax.fori_loop(0, count, step, 0, unroll=unroll)


def kernel(
    n,
    ny,
    *refs,
):
    inputs, (out, *landing), refs = refs[:12], refs[12:25], refs[25:]
    (
        cell,
        w_filter,
        w_gate,
        bias_filter,
        bias_gate,
        adjacency,
        out_block,
        out_dev,
        out_target,
        out_tiles,
        w_mix,
        bias_mix,
    ) = landing
    (
    gated,
    first,
    halo_rows,
    halo_cols,
    send_buf,
    recv_buf,
    target_send,
    target_recv,
    select,
    tiles,
    edge_tiles,
    spread,
    edge_spread,
    table,
    bias_table,
    acc,
    base,
    send_sem,
    recv_sem,
    target_send_sem,
    target_recv_sem,
    halo_send_sem,
    halo_recv_sem,
    fetch_sem,
    route,
    ) = refs
    fetches = [
        pltpu.make_async_copy(src, dst, fetch_sem.at[k])
        for k, (src, dst) in enumerate(zip(inputs, landing))
    ]
    for k in (6, 7, 8, 1, 2, 3, 4, 9, 0, 10, 11, 5):
        fetches[k].start()
    br, bc, size, feats = cell.shape
    blocks = br * bc
    rows = blocks * size
    half = size // 2
    edges = out_tiles.shape[2]
    channels = w_filter.shape[1]
    steps = feats // channels
    stride = edge_spread.shape[0] // half
    rx = lax.axis_index("rx")
    ry = lax.axis_index("ry")

    barrier = pltpu.get_barrier_semaphore()

    def greet(k):
        pl.semaphore_signal(
            barrier, inc=1, device_id={"rx": lax.rem(rx + k + 1, n)}, device_id_type=MESH
        )

    each(n - 1, greet)

    @pl.when(ry > 0)
    def _():
        pl.semaphore_signal(barrier, inc=1, device_id={"ry": ry - 1}, device_id_type=MESH)

    @pl.when(ry < ny - 1)
    def _():
        pl.semaphore_signal(barrier, inc=1, device_id={"ry": ry + 1}, device_id_type=MESH)

    def halo_copies(signal, hop):
        sides = []
        for which, (axis, here, count, halo) in enumerate(
            (("rx", rx, n, halo_rows), ("ry", ry, ny, halo_cols))
        ):
            last = (br if which == 0 else bc) - 1
            for side, (edge, step) in enumerate(((last, 1), (0, -1))):
                src = signal.at[edge] if which == 0 else signal.at[:, edge]
                copy = pltpu.make_async_remote_copy(
                    src_ref=src,
                    dst_ref=halo.at[2 - hop if which == 0 else hop, side],
                    send_sem=halo_send_sem.at[hop, which, side],
                    recv_sem=halo_recv_sem.at[hop, which, side],
                    device_id={axis: jnp.clip(here + step, 0, count - 1)},
                    device_id_type=MESH,
                )
                sends = (here < count - 1) if step == 1 else (here > 0)
                gets = (here > 0) if step == 1 else (here < count - 1)
                sides.append((sends, gets, copy))
        return sides

    def start_halo(signal, hop, axes=(0, 1)):
        for which in axes:
            for sends, gets, copy in halo_copies(signal, hop)[2 * which : 2 * which + 2]:
                pl.when(sends)(copy.start)

    def wait_halo(signal, hop, axes=(0, 1)):
        for which in axes:
            for sends, gets, copy in halo_copies(signal, hop)[2 * which : 2 * which + 2]:
                pl.when(gets)(copy.wait_recv)

    pl.semaphore_wait(
        barrier,
        n - 1 + jnp.where(ry > 0, 1, 0) + jnp.where(ry < ny - 1, 1, 0),
    )

    zero_side = jnp.zeros((2,) + halo_rows.shape[2:], BF16)

    @pl.when(rx == 0)
    def _():
        halo_rows[1:, 0] = zero_side

    @pl.when(rx == n - 1)
    def _():
        halo_rows[1:, 1] = zero_side

    @pl.when(ry == 0)
    def _():
        halo_cols[:, 0] = zero_side

    @pl.when(ry == ny - 1)
    def _():
        halo_cols[:, 1] = zero_side

    start_halo(inputs[0], 0, (0,))
    for k in range(1, 5):
        fetches[k].wait()

    table[...] = jnp.zeros_like(table)
    for t in range(steps):
        span = slice(t * channels, (t + 1) * channels)
        for which, weights in enumerate((w_filter, w_gate)):
            for tap, to in ((1, t), (0, t + DILATION_STEP)):
                if to < steps:
                    at = which * feats + to * channels
                    table[span, at : at + channels] = weights[tap].astype(F32)
        bias_table[0:1, span] = bias_filter[...]
        bias_table[1:2, span] = bias_gate[...]
    taps = table[:, : 2 * feats].astype(BF16)

    def gate(block_rows):
        pre = dot(block_rows, taps)
        pre_f = pre[:, :feats] + bias_table[0:1]
        pre_g = pre[:, feats:] + bias_table[1:2]
        value = jnp.tanh(pre_f) * (0.5 * jnp.tanh(0.5 * pre_g) + 0.5)
        return value.astype(BF16)

    for k in range(6, 10):
        fetches[k].wait()

    for r in range(half):
        piece = out_tiles[0, 0, :, r * 2 * size : (r + 1) * 2 * size]
        edge_spread[r * stride : r * stride + edges] = piece.astype(F32)
    for e in range(edges):
        pairs = edge_spread[pl.ds(e, half, stride=stride), :]
        edge_tiles[e, :half] = pairs.astype(BF16)
        edge_tiles[e, half:] = pltpu.roll(pairs, size, 1).astype(BF16)

    part = n // 2

    def destination(k):
        side = (rx // part + 1 + k % 2) % 2
        return side * part + (rx % part + k // 2 + 1) % part

    lane = lax.broadcasted_iota(jnp.int32, (1, CAP * size), 1)

    def far_copy(hop, d, source):
        return pltpu.make_async_remote_copy(
            src_ref=send_buf.at[hop, d],
            dst_ref=recv_buf.at[hop, source],
            send_sem=send_sem.at[hop, d],
            recv_sem=recv_sem.at[hop, source],
            device_id={"rx": d},
            device_id_type=MESH,
        )

    def target_copy(d, source):
        return pltpu.make_async_remote_copy(
            src_ref=target_send.at[d],
            dst_ref=target_recv.at[source],
            send_sem=target_send_sem.at[d],
            recv_sem=target_recv_sem.at[source],
            device_id={"rx": d},
            device_id_type=MESH,
        )

    def find_route(k):
        d = destination(k)
        head, tail = jnp.int32(-1), jnp.int32(-1)
        for e in range(edges):
            hit = out_dev[0, 0, e] == d
            head = jnp.where(hit & (head < 0), e, head)
            tail = jnp.where(hit, e, tail)
        found = ((head, head >= 0), (tail, tail != head))
        for c, (index, valid) in enumerate(found):
            index = jnp.maximum(index, 0)
            route[k, c] = index
            route[k, CAP + c] = out_block[0, 0, index]
            route[k, 2 * CAP + c] = jnp.where(valid, 1, 0)

    def send_targets(k, own):
        d = destination(k)
        names = [
            jnp.where(route[k, 2 * CAP + c] == 1, out_target[0, 0, route[k, c]], -1)
            for c in range(CAP)
        ]
        named = jnp.where(lane < size, names[0], names[1]).astype(F32)
        if own:
            target_recv[rx] = named
        else:
            target_send[d] = named
            target_copy(d, rx).start()

    team = 2

    def send_group(signal, hop, start, last):
        ks = [start + g for g in range(team)]
        picked = []
        for k in ks:
            for c in range(CAP):
                b = route[k, CAP + c]
                picked.append(signal[lax.div(b, bc), lax.rem(b, bc)])
        sums = []
        for g, k in enumerate(ks):
            for c in range(CAP):
                product = dot(edge_tiles[route[k, c]][:, :size], picked[g * CAP + c])
                sums.append((product * route[k, 2 * CAP + c].astype(F32)).astype(BF16))
        for g, k in enumerate(ks):
            both = jnp.concatenate(sums[g * CAP : (g + 1) * CAP], axis=0)
            if last and g == team - 1:
                recv_buf[hop, rx] = both
            else:
                send_buf[hop, destination(k)] = both
        for g, k in enumerate(ks):
            if not (last and g == team - 1):
                far_copy(hop, destination(k), rx).start()

    def send_far(signal, hop):
        each(n // team - 1, lambda g: send_group(signal, hop, g * team, False))
        send_group(signal, hop, n - team, True)

    part_pairs = n // 4

    def add_far(hop, finish):
        strip = bc * size

        def wait_source(source):
            far_copy(hop, source, source).wait_recv()

        def one(q):
            side = (rx // part + q // part_pairs) % 2
            pair = side * part_pairs + (rx % part // 2 + q % part_pairs) % part_pairs
            if isinstance(q, int) and q == 0:
                wait_source(rx + 1 - 2 * (rx % 2))
            else:
                wait_source(2 * pair)
                wait_source(2 * pair + 1)
            landed = recv_buf[hop, pl.ds(2 * pair, 2)].reshape(2 * CAP * size, feats)
            for i in (0, br - 1, *range(1, br - 1)):
                span = slice(i * strip, (i + 1) * strip)
                total = acc[span] + dot(select[pair, span], landed)
                if isinstance(q, int) and q == n // 2 - 1:
                    finish(i, total)
                else:
                    acc[span] = total

        one(0)
        each(n // 2 - 2, lambda q: one(q + 1))
        one(n // 2 - 1)

    def near(signal, hop):
        for i in range(br):
            for j in range(bc):
                up = signal[i - 1, j] if i > 0 else halo_rows[hop, 0, j]
                down = signal[i + 1, j] if i < br - 1 else halo_rows[hop, 1, j]
                left = signal[i, j - 1] if j > 0 else halo_cols[hop, 0, i]
                right = signal[i, j + 1] if j < bc - 1 else halo_cols[hop, 1, i]
                column = jnp.concatenate([signal[i, j], up, down, left, right], axis=0)
                total = dot(tiles[i * bc + j][:, : 5 * size], column)
                at = (i * bc + j) * size
                acc[pl.ds(at, half, stride=2), :] = total[:half]
                acc[pl.ds(at + 1, half, stride=2), :] = total[half:]

    each(n, find_route)
    each(n - 1, lambda k: send_targets(k, False))
    send_targets(n - 1, True)
    fetches[0].wait()
    for i in range(br):
        gated[i] = gate(cell[i].reshape(bc * size, feats)).reshape(bc, size, feats)
    start_halo(gated, 0, (1,))
    send_far(gated, 0)

    low = lax.broadcasted_iota(jnp.int32, (half, 2 * size), 1) < size

    def arrange(i):
        slot = lax.rem(i, spread.shape[0])
        for k in range(5):
            for r in range(half):
                piece = adjacency[i, k, :, r * 2 * size : (r + 1) * 2 * size]
                at = r * 8 + k % 2 * bc
                spread[slot, k // 2, at : at + bc] = piece.astype(F32)
        for j in range(bc):
            pairs = [
                spread[slot, k // 2, pl.ds(k % 2 * bc + j, half, stride=8), :] for k in range(5)
            ]
            turned = [pltpu.roll(pair, size, 1) for pair in pairs]
            zero = jnp.zeros_like(pairs[0])
            pairs.append(zero)
            turned.append(zero)
            for k in range(0, 6, 2):
                span = slice(k * size, (k + 2) * size)
                even = jnp.where(low, pairs[k], turned[k + 1])
                odd = jnp.where(low, turned[k], pairs[k + 1])
                tiles[i * bc + j, :half, span] = even.astype(BF16)
                tiles[i * bc + j, half:, span] = odd.astype(BF16)

    fetches[5].wait()
    blocks_loop(br, arrange, 2)

    wait_halo(inputs[0], 0, (0,))
    for side, inside in enumerate((rx > 0, rx < n - 1)):
        values = gate(halo_rows[2, side].reshape(bc * size, feats))
        kept = values * jnp.where(inside, 1.0, 0.0).astype(BF16)
        halo_rows[0, side] = kept.reshape(bc, size, feats)
    wait_halo(gated, 0, (1,))
    near(gated, 0)

    def wait_target(k):
        source = lax.rem(rx + n - k - 1, n)
        target_copy(source, source).wait_recv()

    each(n - 1, wait_target)
    spot = lax.broadcasted_iota(jnp.int32, (size, CAP * size), 1) % size
    row = lax.broadcasted_iota(jnp.int32, (size, CAP * size), 0)
    unit = jnp.where(row == 2 * (spot % half) + spot // half, 1.0, 0.0).astype(BF16)
    for source in range(n):
        named = target_recv[source, 0:1]
        span = slice(source % 2 * CAP * size, (source % 2 + 1) * CAP * size)
        for block in range(blocks):
            hit = jnp.where(named == float(block), 1.0, 0.0).astype(BF16)
            select[source // 2, block * size : (block + 1) * size, span] = unit * hit

    strip = bc * size

    def end_first(i, total):
        first[i] = total.astype(BF16).reshape(bc, size, feats)
        if i == br - 1:
            start_halo(first, 1, (0,))

    add_far(0, end_first)
    start_halo(first, 1, (1,))
    send_far(first, 1)

    for k in (10, 11):
        fetches[k].wait()
    for t in range(steps):
        span = slice(t * channels, (t + 1) * channels)
        for hop in range(3):
            at = (2 + hop) * feats + t * channels
            table[span, at : at + channels] = w_mix[hop].astype(F32)
        bias_table[2:3, span] = bias_mix[...]
    mixes = [table[:, (2 + h) * feats : (3 + h) * feats].astype(BF16) for h in range(3)]
    early_mix = jnp.concatenate(mixes[:2], axis=0)
    late_mix = jnp.concatenate([mixes[2], mixes[2]], axis=0)

    for i in range(br):
        known = [gated[i].reshape(strip, feats), first[i].reshape(strip, feats)]
        own = dot(jnp.concatenate(known, axis=1), early_mix) + bias_table[2:3]
        base[i * strip : (i + 1) * strip] = own + cell[i].reshape(strip, feats).astype(F32)
    wait_halo(first, 1)
    near(first, 1)

    def end_second(i, second):
        upper = second.astype(BF16)
        lower = (second - upper.astype(F32)).astype(BF16)
        total = base[i * strip : (i + 1) * strip]
        total = total + dot(jnp.concatenate([upper, lower], axis=1), late_mix)
        out[i] = total.astype(BF16).reshape(bc, size, feats)

    add_far(1, end_second)

    for hop, signals in enumerate(((inputs[0], gated), (first, first))):
        for which in range(2):
            for sends, gets, copy in halo_copies(signals[which], hop)[2 * which : 2 * which + 2]:
                pl.when(sends)(copy.wait_send)

        def sent(k):
            d = destination(k)
            far_copy(hop, d, rx).wait_send()
            if hop == 0:
                target_copy(d, rx).wait_send()

        each(n - 1, sent)


def local(
    n,
    ny,
    cell_input,
    w_filter,
    w_gate,
    bias_filter,
    bias_gate,
    adjacency,
    out_block,
    out_dev,
    out_target,
    out_tiles,
    w_mix,
    bias_mix,
):
    br, bc, size, feats = cell_input.shape
    blocks = br * bc
    rows = blocks * size
    edges = out_tiles.shape[2]
    channels = w_filter.shape[1]
    half = size // 2
    stride = -(-edges // 8) * 8
    assert feats == 128 and size == 64 and br == bc == 4 and n % 4 == 0
    vmem = pl.BlockSpec(memory_space=pltpu.VMEM)
    dma = pltpu.SemaphoreType.DMA
    hbm = pl.BlockSpec(memory_space=pltpu.HBM)
    operands = (
        cell_input,
        w_filter,
        w_gate,
        bias_filter.reshape(1, channels),
        bias_gate.reshape(1, channels),
        adjacency.transpose(0, 2, 1, 3),
        out_block,
        out_dev.reshape(out_block.shape),
        out_target,
        out_tiles,
        w_mix,
        bias_mix.reshape(1, channels),
    )
    scratch = [
        (pltpu.SMEM if k in (6, 7, 8) else pltpu.VMEM)(a.shape, a.dtype)
        for k, a in enumerate(operands)
    ] + [
        pltpu.VMEM((br, bc, size, feats), BF16),
        pltpu.VMEM((br, bc, size, feats), BF16),
        pltpu.VMEM((3, 2, bc, size, feats), BF16),
        pltpu.VMEM((2, 2, br, size, feats), BF16),
        pltpu.VMEM((2, n, CAP * size, feats), BF16),
        pltpu.VMEM((2, n, CAP * size, feats), BF16),
        pltpu.VMEM((n, 1, CAP * size), F32),
        pltpu.VMEM((n, 1, CAP * size), F32),
        pltpu.VMEM((n // 2, rows, 2 * CAP * size), BF16),
        pltpu.VMEM((blocks, size, 6 * size), BF16),
        pltpu.VMEM((edges, size, 2 * size), BF16),
        pltpu.VMEM((2, 3, half * 8, 2 * size), F32),
        pltpu.VMEM((half * stride, 2 * size), F32),
        pltpu.VMEM((feats, 5 * feats), F32),
        pltpu.VMEM((8, feats), F32),
        pltpu.VMEM((rows, feats), F32),
        pltpu.VMEM((rows, feats), F32),
        dma((2, n)),
        dma((2, n)),
        dma((n,)),
        dma((n,)),
        dma((2, 2, 2)),
        dma((2, 2, 2)),
        dma((12,)),
        pltpu.SMEM((n, 3 * CAP), jnp.int32),
    ]
    near_flops = 2 * 2 * 5 * rows * size * feats
    return pl.pallas_call(
        functools.partial(kernel, n, ny),
        out_shape=jax.ShapeDtypeStruct(cell_input.shape, BF16),
        in_specs=[hbm] * 12,
        out_specs=vmem,
        scratch_shapes=scratch,
        cost_estimate=pl.CostEstimate(
            flops=near_flops, bytes_accessed=2 * rows * feats * 2, transcendentals=2 * rows * feats
        ),
        compiler_params=pltpu.CompilerParams(
            collective_id=0, has_side_effects=True, vmem_limit_bytes=40 * 1024 * 1024
        ),
    )(*(pltpu.with_memory_space_constraint(a, pltpu.HBM) for a in operands))


def solution(mesh):
    in_specs = (
        P("rx", "ry", None, None),
        P(),
        P(),
        P(),
        P(),
        P("rx", "ry", None, None),
        P("rx", "ry", None),
        P("rx", "ry", None, None),
        P("rx", "ry", None),
        P("rx", "ry", None, None),
        P(),
        P(),
    )
    out_specs = P("rx", "ry", None, None)
    body = functools.partial(local, mesh.shape["rx"], mesh.shape["ry"])
    return jax.shard_map(body, mesh=mesh, in_specs=in_specs, out_specs=out_specs, check_vma=False)
```
